32 devices in a mesh: dp: 4 (over x, core), chan: 2 (over y), ctx: 4 (over z).
Axes of the slice: x: 2, y: 2, z: 4, core: 2. Of those that a mesh axis runs over, the one named last changes fastest.
Arguments:
- query_proj: bfloat16 [4, 512, 4096], P('dp', 'ctx', 'chan'), may hold values from -6 to 6
- key_proj: bfloat16 [4, 512, 4096], P('dp', 'ctx', 'chan'), may hold values from -6 to 6
- value_proj: bfloat16 [4, 512, 4096], P('dp', 'ctx', 'chan'), may hold values from -6 to 6
- out_grad: bfloat16 [4, 512, 4096], P('dp', 'ctx', 'chan'), may hold values from -6 to 6
- filter_taps: float32 [4096, 512], P(('chan', 'ctx')), may hold values from -0.25 to 0.25
Outputs:
- grad_q: bfloat16 [4, 512, 4096], P('dp', 'ctx', 'chan')
- grad_k: bfloat16 [4, 512, 4096], P('dp', 'ctx', 'chan')
- grad_v: bfloat16 [4, 512, 4096], P('dp', 'ctx', 'chan')
- grad_filt: float32 [4096, 512], P(('chan', 'ctx'))
The draws below stay inside these ranges and needn't reach their ends.
All inputs are finite; a program needn't handle non-finite values.
Results may differ from the reference program's by a relative error of at most 0.014.
Values may be sent and summed in bfloat16 or wider, within the bound.
No kernel may reach another device: no remote copies, remote signals or barrier semaphores. Data moves between devices by JAX's collectives and lax.ppermute only.
A program may use at most 64 MiB of HBM per device.

```python
import math
import jax
import jax.numpy as jnp
from jax import lax

D = 4096
SEQS = 4
L = 512


def level_of(key, extent, shards, smallest, high):
    gain = 1.0
    for dim, shards_of in shards:
        draws = jax.random.uniform(jax.random.fold_in(jax.random.fold_in(key, 6), dim), (shards_of,), jnp.float32, smallest / len(shards), high / len(shards))
        gain = gain * jnp.repeat(jnp.exp(draws), extent[dim] // shards_of).reshape((-1,) + (1,) * (len(extent) - 1 - dim))
    return gain


def gaussian(stream_key, shape, scale, most, pieces=(), held_as=jnp.bfloat16):
    entries = jax.random.normal(stream_key, shape, jnp.float32) * scale
    if len(pieces) > 0:
        entries = level_of(stream_key, shape, pieces, -0.22, 0.18) * entries
    return jnp.clip(entries, min=-most, max=most).astype(held_as)


def setup_inputs(seed: int = 0) -> dict:
    keys = jax.random.split(jax.random.key(seed), 6)
    query_proj = gaussian(keys[0], (SEQS, L, D), 1.0, 6.0, ((0, 4), (1, 4), (2, 2)))
    key_proj = gaussian(keys[1], (SEQS, L, D), 1.0, 6.0, ((0, 4), (1, 4), (2, 2)))
    value_proj = gaussian(keys[2], (SEQS, L, D), 1.0, 6.0, ((0, 4), (1, 4), (2, 2)))
    out_grad = gaussian(keys[3], (SEQS, L, D), 1.0, 6.0, ((0, 4), (1, 4), (2, 2)))
    filter_taps = gaussian(keys[4], (D, L), L ** -0.5, 0.25, ((0, 8),), jnp.float32)
    return {"query_proj": query_proj, "key_proj": key_proj, "value_proj": value_proj, "out_grad": out_grad, "filter_taps": filter_taps}


def channel_block(inputs):
    gated_blk, grad_blk, taps_blk = inputs
    length = taps_blk.shape[1]
    padded = 2 * length
    gate_spec = jnp.fft.rfft(gated_blk.astype(jnp.float32), n=padded, axis=1)
    grad_spec = jnp.fft.rfft(grad_blk.astype(jnp.float32), n=padded, axis=1)
    filt_spec = jnp.fft.rfft(taps_blk.astype(jnp.float32), n=padded, axis=1).T[None]
    conv_out = jnp.fft.irfft(gate_spec * filt_spec, n=padded, axis=1)[:, :length].astype(jnp.bfloat16)
    back_conv = jnp.fft.irfft(grad_spec * jnp.conj(filt_spec), n=padded, axis=1)[:, :length].astype(jnp.bfloat16)
    cross_corr = jnp.fft.irfft(jnp.conj(gate_spec) * grad_spec, n=padded, axis=1)[:, :length]
    return conv_out, back_conv, jnp.sum(cross_corr, axis=0).T


def reference(query_proj, key_proj, value_proj, out_grad, filter_taps):
    seq_count, length, channels = query_proj.shape
    block_size = math.gcd(channels, 512)
    block_count = channels // block_size
    query_vals = query_proj.astype(jnp.float32)
    key_vals = key_proj.astype(jnp.float32)
    grad_vals = out_grad.astype(jnp.float32)
    gated = (query_vals * key_vals).astype(jnp.bfloat16)
    grad_conv = (grad_vals * value_proj.astype(jnp.float32)).astype(jnp.bfloat16)

    def split_blocks(values):
        return values.reshape(seq_count, length, block_count, block_size).transpose(2, 0, 1, 3)

    def join_blocks(values):
        return values.transpose(1, 2, 0, 3).reshape(seq_count, length, channels)

    conv_out, back_conv, grad_filt = lax.map(
        channel_block,
        (split_blocks(gated), split_blocks(grad_conv), filter_taps.reshape(block_count, block_size, length)))
    conv_out = join_blocks(conv_out)
    back_vals = join_blocks(back_conv).astype(jnp.float32)
    grad_q = (back_vals * key_vals).astype(jnp.bfloat16)
    grad_k = (back_vals * query_vals).astype(jnp.bfloat16)
    grad_v = (grad_vals * conv_out.astype(jnp.float32)).astype(jnp.bfloat16)
    return grad_q, grad_k, grad_v, grad_filt.reshape(channels, length)
```

```python
import functools
import math

import jax
import jax.numpy as jnp
import ml_dtypes
import numpy as np
from jax import lax
from jax.experimental import pallas as pl
from jax.experimental.pallas import tpu as pltpu
from jax.sharding import PartitionSpec as P

bf16 = jnp.bfloat16
f32 = jnp.float32
VMEM_LIMIT = 48 * 1024 * 1024


def dft_table(size):
    freq = np.arange(size // 2)[:, None]
    pos = np.arange(-size // 2, size // 2)[None, :]
    angle = 2.0 * np.pi * (((2 * freq + 1) * pos) % (2 * size)) / (2 * size)
    return np.concatenate([np.cos(angle), -np.sin(angle)], 0)


def as_const(table):
    return jnp.asarray(np.ascontiguousarray(table).astype(ml_dtypes.bfloat16))


def mm(left, right, dims=((1,), (0,))):
    return lax.dot_general(left, right, (dims, ((), ())), preferred_element_type=f32)


def cmul(left, right):
    half = left.shape[0] // 2
    lr, li, rr, ri = left[:half], left[half:], right[:half], right[half:]
    return lr * rr - li * ri, lr * ri + li * rr


def cmulc(left, right):
    half = left.shape[0] // 2
    lr, li, rr, ri = left[:half], left[half:], right[:half], right[half:]
    return lr * rr + li * ri, lr * ri - li * rr


def join(pair):
    return jnp.concatenate([pair[0], pair[1]], 0)


def lanes(start, width):
    return pl.ds(pl.multiple_of(start, 128), width)


def call(kernel, outs, n_in, smem_first=True, cost=(0, 0), specs=None, limit=VMEM_LIMIT):
    vmem = pl.BlockSpec(memory_space=pltpu.VMEM)
    in_specs = [vmem] * n_in if specs is None else specs
    if smem_first:
        in_specs = [pl.BlockSpec(memory_space=pltpu.SMEM)] + in_specs
    return pl.pallas_call(
        kernel,
        out_shape=[jax.ShapeDtypeStruct(s, d) for s, d in outs],
        in_specs=in_specs,
        out_specs=[vmem] * len(outs),
        compiler_params=pltpu.CompilerParams(vmem_limit_bytes=limit),
        cost_estimate=pl.CostEstimate(flops=cost[0], bytes_accessed=cost[1], transcendentals=0),
    )


def gate_kernel(chunks, quarter, idx, q, k, v, g, *outs):
    z, upper = idx[0], idx[2]
    width = quarter // chunks
    for c in range(chunks):
        keep, to1, to2, to3 = outs[4 * c : 4 * c + 4]
        for r in range(4):
            cols = lanes((z ^ r) * quarter + c * width, width)
            gated = (q[0, :, cols].astype(f32) * k[0, :, cols].astype(f32)).astype(bf16)
            grad = (g[0, :, cols].astype(f32) * v[0, :, cols].astype(f32)).astype(bf16)
            dest, slot = (keep, r // 2) if r in (0, 2) else (to1, r // 2)
            dest[0, slot] = gated
            dest[1, slot] = grad
            if r >= 2:
                sel = jnp.where(upper == 0, gated.astype(f32), grad.astype(f32)).astype(bf16)
                (to2 if r == 2 else to3)[...] = sel


def own_filter_kernel(table, taps, near, cross):
    half = taps.shape[1] // 2
    vals = taps[...].astype(bf16)
    cross[...] = mm(table[...], vals, ((1,), (1,)))
    near[...] = mm(table[:, half:], vals[:, :half], ((1,), (1,)))


def other_filter_kernel(idx, table, mine, across, near):
    dp = idx[3]
    half = table.shape[1] // 2
    rows = mine.shape[0] // 2
    for j in range(4):
        piece = (mine if j < 2 else across)[(j % 2) * rows : (j % 2 + 1) * rows, :]
        near[:, lanes((dp ^ j) * rows, rows)] = mm(table[:, half:], piece, ((1,), (1,)))


def conv_kernel(first, width, idx, fwd, inv, near, cross, other, keep, r1, r2, r3,
                okeep, o1, o2, o3, q_near, q_cross, q_other):
    low, upper = idx[1], idx[2]
    cols = slice(first, first + width)
    table = fwd[low]
    back_table = inv[low]
    block = keep.shape[2]

    def spec(top, bottom):
        return mm(table, jnp.concatenate([top, bottom], 0))

    def inverse(pair):
        return mm(back_table, join(pair).astype(bf16)).astype(bf16)

    def put(kind, slot, pair):
        vals = inverse(pair)
        okeep[kind, slot] = vals[:block]
        o1[kind, slot] = vals[block:]

    x1, g1 = spec(keep[0, 1], r1[0, 1]), spec(keep[1, 1], r1[1, 1])
    h1 = other[:, cols]
    put(0, 1, cmul(x1, h1))
    put(1, 1, cmulc(h1, g1))
    q_other[...] = join(cmulc(x1, g1)).astype(bf16)

    x0, g0 = spec(keep[0, 0], r1[0, 0]), spec(keep[1, 0], r1[1, 0])
    rec = spec(r2[...], r3[...])
    h0 = near[:, cols]
    hx = cross[:, cols]
    half = hx.shape[0] // 2
    sign = jnp.where(upper == 0, 1.0, -1.0)
    is_up = jnp.where(upper == 0, 0.0, 1.0)
    hx = jnp.concatenate([hx[:half], hx[half:] * sign], 0)
    own = jnp.where(upper == 0, x0, g0)
    vals = inverse(cmul(own, hx))
    o2[...] = vals[:block]
    o3[...] = vals[block:]
    add = cmulc(hx, rec)
    conv = cmul(x0, h0)
    back = cmulc(h0, g0)
    put(0, 0, (conv[0] + is_up * add[0], conv[1] + is_up * add[1]))
    put(1, 0, (back[0] + (1.0 - is_up) * add[0], back[1] + (1.0 - is_up) * add[1]))
    q_near[...] = join(cmulc(x0, g0)).astype(bf16)
    qc = cmulc(own, rec)
    q_cross[...] = join((qc[0], qc[1] * sign)).astype(bf16)


def filt_kernel(idx, table, q_near, q_cross, q_other, keep_own, keep_far, send_own, send_far):
    core = idx[3] & 1
    half = table.shape[1] // 2
    width = q_near.shape[1] // 2
    scale = 1.0 / half
    lo, hi = table[:, :half], table[:, half:]
    tn = ((0,), (0,))
    for own, far, which in ((send_own, send_far, 1 - core), (keep_own, keep_far, core)):
        cols = lanes(which * width, width)
        qn, qc, qo = q_near[:, cols], q_cross[:, cols], q_other[:, cols]
        far[...] = (mm(qo, hi, tn) * scale).astype(far.dtype)
        own[:, :half] = ((mm(qc, lo, tn) + mm(qn, hi, tn)) * scale).astype(own.dtype)
        own[:, half:] = (mm(qc, hi, tn) * scale).astype(own.dtype)


def final_kernel(chunks, quarter, idx, q, k, g, *refs):
    z, upper, core = idx[0], idx[2], idx[3] & 1
    dq, dk, dv, grad_filt = refs[-4:]
    filt = refs[4 * chunks : -4]
    per = len(filt) // chunks // 2
    for c in range(chunks):
        for j in range(2 * per):
            piece = filt[2 * per * c + j]
            rows = piece.shape[0]
            which = core if j < per else 1 - core
            start = pl.multiple_of((2 * c + which) * per * rows + (j % per) * rows, 8)
            grad_filt[pl.ds(start, rows), :] = piece[...].astype(f32)
    width = quarter // chunks
    is_up = jnp.where(upper == 0, 0.0, 1.0)
    for c in range(chunks):
        keep, r1, r2, r3 = refs[4 * c : 4 * c + 4]
        for r in range(4):
            cols = lanes((z ^ r) * quarter + c * width, width)
            src = keep if r in (0, 2) else r1
            conv = src[0, r // 2].astype(f32)
            back = src[1, r // 2].astype(f32)
            if r >= 2:
                add = (r2 if r == 2 else r3)[...].astype(f32)
                conv = conv + is_up * add
                back = back + (1.0 - is_up) * add
            dv[0, :, cols] = (g[0, :, cols].astype(f32) * conv).astype(bf16)
            dq[0, :, cols] = (back * k[0, :, cols].astype(f32)).astype(bf16)
            dk[0, :, cols] = (back * q[0, :, cols].astype(f32)).astype(bf16)


def half_plan(chunks, query_proj, key_proj, value_proj, out_grad, filter_taps):
    z = lax.axis_index("ctx").astype(jnp.int32)
    dp = lax.axis_index("dp").astype(jnp.int32)
    idx = jnp.stack([z, z & 1, z >> 1, dp])
    block, group = query_proj.shape[1:]
    quarter, length = filter_taps.shape
    width = quarter // chunks
    half = length // 2
    table = dft_table(length)
    near_cols = table[:, half:]
    swapped = np.concatenate([near_cols[:, block:], near_cols[:, :block]], 1)
    table_c = as_const(table)
    fwd = as_const(np.stack([near_cols, swapped]))
    inv = as_const(np.stack([near_cols.T, swapped.T]) / half)

    def xz(vals, k):
        return lax.ppermute(vals, "ctx", [(i, i ^ k) for i in range(4)])

    def xd(vals, k):
        return lax.ppermute(vals, "dp", [(i, i ^ k) for i in range(4)])

    def apart(run, *args):
        shapes = jax.eval_shape(run, *args)
        return lax.cond(dp >= 0, run, lambda *_: jax.tree.map(lambda s: jnp.zeros(s.shape, s.dtype), shapes), *args)

    share = quarter // 4
    piece0 = xz(lax.dynamic_slice(filter_taps, (dp * share, 0), (share, half)).astype(bf16), 2)
    msg = (2, 2, block, width)
    gate_outs = [(msg, bf16), (msg, bf16), ((block, width), bf16), ((block, width), bf16)] * chunks
    sent = call(
        functools.partial(gate_kernel, chunks, quarter),
        gate_outs,
        4,
        cost=(2 * block * group, 16 * block * group),
        limit=63 * 1024 * 1024,
    )(idx, query_proj, key_proj, value_proj, out_grad)
    got = []
    for c in range(chunks):
        keep, to1, to2, to3 = sent[4 * c : 4 * c + 4]
        got.append((keep, xz(to1, 1), xz(to2, 2), xz(to3, 3)))

    piece1 = xd(piece0, 1)

    def filters(piece0, piece1, filter_taps, idx):
        spec_shape = ((length, quarter), f32)
        near, cross = call(own_filter_kernel, [spec_shape] * 2, 2, smem_first=False, cost=(3 * length * half * quarter * 2, 4 * length * quarter * 4))(
            table_c, filter_taps
        )
        pair = jnp.concatenate([piece0, piece1], 0)
        (other,) = call(other_filter_kernel, [spec_shape], 3, cost=(length * half * quarter * 2, 2 * length * quarter * 4))(
            idx, table_c, pair, xd(pair, 2)
        )
        return near, cross, other

    near, cross, other = apart(filters, piece0, piece1, filter_taps, idx)
    spec_b = ((length, width), bf16)
    done = []
    spectra = []
    for c in range(chunks):
        outs = call(
            functools.partial(conv_kernel, c * width, width),
            gate_outs[:4] + [spec_b] * 3,
            9,
            cost=(10 * length * half * width * 2, 30 * block * width * 2 + 12 * length * width * 4),
        )(idx, fwd, inv, near, cross, other, *got[c])
        okeep, o1, o2, o3 = outs[:4]
        done += [okeep, xz(o1, 1), xz(o2, 2), xz(o3, 3)]
        spectra.append(outs[4:])

    def filter_grad(spectra, idx):
        filt = []
        rows = width // 2
        shapes = [((rows, length), f32), ((rows, half), f32), ((rows, length), bf16), ((rows, half), bf16)]

        def summed(keep, send):
            chip = lax.reduce_precision(keep + xd(send, 1).astype(f32), 8, 7).astype(bf16)
            return chip.astype(f32) + xd(chip, 2).astype(f32)

        for c in range(chunks):
            keep_own, keep_far, send_own, send_far = call(
                filt_kernel, shapes, 4, cost=(4 * length * half * width * 2, 10 * length * width * 2)
            )(idx, table_c, *spectra[c])
            far = xz(summed(keep_far, send_far).astype(bf16), 2).astype(f32)
            own = summed(keep_own, send_own)
            mine = jnp.concatenate([own[:, :half] + far, own[:, half:]], 1).astype(bf16)
            filt += [mine, xd(mine, 1)]
        return filt

    filt = apart(filter_grad, spectra, idx)
    act = (query_proj.shape, bf16)
    return call(
        functools.partial(final_kernel, chunks, quarter),
        [act] * 3 + [(filter_taps.shape, f32)],
        3 + len(done) + len(filt),
        cost=(3 * block * group, 18 * block * group),
    )(idx, query_proj, key_proj, out_grad, *done, *filt)


exact_mode = lax.Precision.HIGHEST
field_mode = lax.Precision.HIGH


def factor_sizes(length):
    col_count = min(128, length)
    return (2 * length // col_count, col_count)


def angle_table(first_size, second_size, period):
    product = (
        jnp.arange(first_size, dtype=jnp.int32)[:, None]
        * jnp.arange(second_size, dtype=jnp.int32)[None, :]
        % period
    )
    angles = product.astype(jnp.float32) * (2.0 * math.pi / period)
    return (jnp.cos(angles), jnp.sin(angles))


def make_tables(length):
    row_count, col_count = factor_sizes(length)
    outer_cos, outer_sin = angle_table(row_count, row_count // 2, row_count)
    twist_cos, twist_sin = angle_table(row_count, col_count, row_count * col_count)
    inner_cos, inner_sin = angle_table(col_count, col_count, col_count)
    real_outer = jnp.stack([outer_cos, -outer_sin])
    mixed_outer = jnp.stack([jnp.stack([outer_cos, outer_sin]), jnp.stack([-outer_sin, outer_cos])])
    fwd_twist = jnp.stack([twist_cos, -twist_sin])[:, None]
    inv_twist = jnp.stack([twist_cos, twist_sin])[:, None]
    fwd_inner = jnp.stack([jnp.stack([inner_cos, -inner_sin]), jnp.stack([inner_sin, inner_cos])])
    inv_inner = jnp.stack([jnp.stack([inner_cos, inner_sin]), jnp.stack([-inner_sin, inner_cos])])
    back_outer = jnp.stack([outer_cos, -outer_sin]) / float(row_count * col_count)
    return (real_outer, mixed_outer, fwd_twist, inv_twist, fwd_inner, inv_inner, back_outer)


def complex_mul(left, right):
    return jnp.stack(
        [left[0] * right[0] - left[1] * right[1], left[0] * right[1] + left[1] * right[0]]
    )


def conjugate(values):
    return jnp.stack([values[0], -values[1]])


def forward(values, tables, mode):
    real_outer, mixed_outer, fwd_twist, inv_twist, fwd_inner, inv_inner, back_outer = tables
    half_rows = real_outer.shape[2]
    col_count = fwd_inner.shape[2]
    grid = values.reshape(values.shape[0], half_rows, col_count)
    first = jnp.einsum("sca,hab->shcb", real_outer, grid, precision=mode)
    turned = complex_mul(first, fwd_twist)
    return jnp.einsum("shcb,stbd->thcd", turned, fwd_inner, precision=mode)


def inverse(spectrum, tables, mode):
    real_outer, mixed_outer, fwd_twist, inv_twist, fwd_inner, inv_inner, back_outer = tables
    back = jnp.einsum("shcd,stdb->thcb", spectrum, inv_inner, precision=mode)
    turned = complex_mul(back, inv_twist)
    out_grid = jnp.einsum("sca,shcb->hab", back_outer, turned, precision=mode)
    return out_grid.reshape(out_grid.shape[0], -1)


def whole_plan(query_proj, key_proj, value_proj, out_grad, filter_taps):
    query_vals = query_proj[0].astype(jnp.float32)
    key_vals = key_proj[0].astype(jnp.float32)
    grad_vals = out_grad[0].astype(jnp.float32)
    gated_vals = (query_vals * key_vals).astype(jnp.bfloat16).T
    grad_conv = (grad_vals * value_proj[0].astype(jnp.float32)).astype(jnp.bfloat16).T
    length = filter_taps.shape[1]
    tables = make_tables(length)
    filt_spec = forward(filter_taps, tables, exact_mode)
    gated_all = lax.all_to_all(gated_vals, "ctx", split_axis=0, concat_axis=1, tiled=True)
    gate_spec = forward(gated_all.astype(jnp.float32), tables, field_mode)
    conv_full = inverse(complex_mul(gate_spec, filt_spec), tables, field_mode).astype(jnp.bfloat16)
    conv_local = lax.all_to_all(conv_full, "ctx", split_axis=1, concat_axis=0, tiled=True)
    grad_all = lax.all_to_all(grad_conv, "ctx", split_axis=0, concat_axis=1, tiled=True)
    grad_spec = forward(grad_all.astype(jnp.float32), tables, field_mode)
    back_full = inverse(complex_mul(grad_spec, conjugate(filt_spec)), tables, field_mode).astype(
        jnp.bfloat16
    )
    back_local = lax.all_to_all(back_full, "ctx", split_axis=1, concat_axis=0, tiled=True)
    grad_v = (grad_vals * conv_local.T.astype(jnp.float32)).astype(jnp.bfloat16)[None]
    back_vals = back_local.T.astype(jnp.float32)
    grad_q = (back_vals * key_vals).astype(jnp.bfloat16)[None]
    grad_k = (back_vals * query_vals).astype(jnp.bfloat16)[None]
    cross_spec = complex_mul(conjugate(gate_spec), grad_spec)
    grad_filt = lax.psum(inverse(cross_spec, tables, exact_mode).astype(jnp.bfloat16), "dp").astype(
        jnp.float32
    )
    return (grad_q, grad_k, grad_v, grad_filt)

def solution(mesh):
    split = mesh.shape["ctx"] == 4 and mesh.shape["dp"] == 4
    body = functools.partial(half_plan, 1) if split else whole_plan
    acts = P("dp", "ctx", "chan")
    taps = P(("chan", "ctx"), None)
    return jax.shard_map(
        body,
        mesh=mesh,
        in_specs=(acts, acts, acts, acts, taps),
        out_specs=(acts, acts, acts, taps),
        check_vma=False,
    )
```

```python
import functools
import math

import jax
import jax.numpy as jnp
import ml_dtypes
import numpy as np
from jax import lax
from jax.experimental import pallas as pl
from jax.experimental.pallas import tpu as pltpu
from jax.sharding import PartitionSpec as P

bf16 = jnp.bfloat16
f32 = jnp.float32
VMEM_LIMIT = 20 * 1024 * 1024
CONV_VMEM = 20 * 1024 * 1024
GATE_VMEM = 63 * 1024 * 1024
ROW_CHUNKS = 4


def dft_table(size):
    freq = np.arange(size // 2)[:, None]
    pos = np.arange(-size // 2, size // 2)[None, :]
    angle = 2.0 * np.pi * (((2 * freq + 1) * pos) % (2 * size)) / (2 * size)
    return np.concatenate([np.cos(angle), -np.sin(angle)], 0)


def as_const(table):
    return jnp.asarray(np.ascontiguousarray(table).astype(ml_dtypes.bfloat16))


def mm(left, right, dims=((1,), (0,))):
    return lax.dot_general(left, right, (dims, ((), ())), preferred_element_type=f32)


def cmul(left, right):
    half = left.shape[0] // 2
    lr, li, rr, ri = left[:half], left[half:], right[:half], right[half:]
    return lr * rr - li * ri, lr * ri + li * rr


def cmulc(left, right):
    half = left.shape[0] // 2
    lr, li, rr, ri = left[:half], left[half:], right[:half], right[half:]
    return lr * rr + li * ri, lr * ri - li * rr


def join(pair):
    return jnp.concatenate([pair[0], pair[1]], 0)


def lanes(start, width):
    return pl.ds(pl.multiple_of(start, 128), width)


def call(kernel, outs, n_in, smem_first=True, cost=(0, 0), limit=VMEM_LIMIT, in_hbm=0, out_hbm=False, scratch=()):
    vmem, hbm = pl.BlockSpec(memory_space=pltpu.VMEM), pl.BlockSpec(memory_space=pltpu.HBM)
    in_specs = [hbm] * in_hbm + [vmem] * (n_in - in_hbm)
    if smem_first:
        in_specs = [pl.BlockSpec(memory_space=pltpu.SMEM)] + in_specs
    return pl.pallas_call(
        kernel,
        out_shape=[jax.ShapeDtypeStruct(s, d) for s, d in outs],
        in_specs=in_specs,
        out_specs=[hbm if out_hbm else vmem] * len(outs),
        scratch_shapes=scratch,
        compiler_params=pltpu.CompilerParams(vmem_limit_bytes=limit),
        cost_estimate=pl.CostEstimate(flops=cost[0], bytes_accessed=cost[1], transcendentals=0),
    )


def gate_kernel(quarter, idx, q, k, v, g, taps, keep_own, keep_far, own1, far1, to2, to3, piece):
    z, upper = idx[0], idx[2]
    piece[...] = taps[...].astype(bf16)
    for r, dest in ((3, far1), (2, keep_far), (1, own1), (0, keep_own)):
        cols = lanes((z ^ r) * quarter, quarter)
        gated = (q[0, :, cols].astype(f32) * k[0, :, cols].astype(f32)).astype(bf16)
        grad = (g[0, :, cols].astype(f32) * v[0, :, cols].astype(f32)).astype(bf16)
        dest[0] = gated
        dest[1] = grad
        if r >= 2:
            sel = jnp.where(upper == 0, gated.astype(f32), grad.astype(f32)).astype(bf16)
            (to2 if r == 2 else to3)[...] = sel


def own_filter_kernel(table, taps, near, cross, inv):
    half = taps.shape[1] // 2
    inv[...] = (table[:, half:].astype(f32).T * (1.0 / half)).astype(bf16)
    vals = taps[...].astype(bf16)
    cross[...] = mm(table[...], vals, ((1,), (1,))).astype(bf16)
    near[...] = mm(table[:, half:], vals[:, :half], ((1,), (1,))).astype(bf16)


def in_order(low, mine, partner, held):
    block = mine.shape[0]
    held[pl.ds(pl.multiple_of(low * block, block), block), :] = mine
    held[pl.ds(pl.multiple_of((1 - low) * block, block), block), :] = partner
    return held[...]


def halves(low, vals, held, mine, partner):
    held[...] = vals
    block = vals.shape[0] // 2
    mine[...] = held[pl.ds(pl.multiple_of(low * block, block), block), :]
    partner[...] = held[pl.ds(pl.multiple_of((1 - low) * block, block), block), :]


def filt_part(core, table, terms, keep, send):
    half = table.shape[1] // 2
    width = keep.shape[0]
    for dest, which in ((send, 1 - core), (keep, core)):
        cols = lanes(which * width, width)
        for first, pairs in terms:
            vals = sum(mm(q[:, cols], table[:, start : start + half], ((0,), (0,))) for q, start in pairs)
            dest[:, first : first + half] = (vals * (1.0 / half)).astype(dest.dtype)


def conv_far_kernel(idx, table, inv, mine, across, keep, recv, okeep, o1, gkeep, gsend, filt, q_far, held):
    low, dp = idx[1], idx[3]
    half = table.shape[1] // 2
    share = mine.shape[0] // 2
    fwd = table[:, half:]
    x = mm(fwd, in_order(low, keep[0], recv[0], held.at[0]))
    g = mm(fwd, in_order(low, keep[1], recv[1], held.at[1]))
    for j in range(4):
        piece = (mine if j < 2 else across)[(j % 2) * share : (j % 2 + 1) * share, :]
        filt[:, lanes((dp ^ j) * share, share)] = mm(fwd, piece, ((1,), (1,)))
    h = filt[...]
    q_far[...] = join(cmulc(x, g)).astype(bf16)
    for kind, pair in ((0, cmul(x, h)), (1, cmulc(h, g))):
        halves(low, mm(inv[...], join(pair).astype(bf16)).astype(bf16), held.at[2 + kind], okeep.at[kind], o1.at[kind])
    filt_part(dp & 1, table, [(0, [(q_far, half)])], gkeep, gsend)


def conv_own_kernel(idx, table, inv, near, cross, keep, recv, r2, r3, okeep, o1, o2, o3, gkeep, gsend, q_near, q_cross, held):
    low, upper, core = idx[1], idx[2], idx[3] & 1
    half = table.shape[1] // 2

    def inverse(pair):
        return mm(inv[...], join(pair).astype(bf16)).astype(bf16)

    def run(is_upper):
        fwd = table[:, half:]
        x = mm(fwd, in_order(low, keep[0], recv[0], held.at[0]))
        g = mm(fwd, in_order(low, keep[1], recv[1], held.at[1]))
        rec = mm(fwd, in_order(low, r2[...], r3[...], held.at[2]))
        hx = cross[...].astype(f32)
        halves(low, inverse(cmulc(hx, g) if is_upper else cmul(hx, x)), held.at[3], o2, o3)
        add = cmul(hx, rec) if is_upper else cmulc(hx, rec)
        h = near[...].astype(f32)
        conv = cmul(x, h)
        back = cmulc(h, g)
        if is_upper:
            conv = (conv[0] + add[0], conv[1] + add[1])
        else:
            back = (back[0] + add[0], back[1] + add[1])
        halves(low, inverse(conv), held.at[4], okeep.at[0], o1.at[0])
        halves(low, inverse(back), held.at[5], okeep.at[1], o1.at[1])
        q_near[...] = join(cmulc(x, g)).astype(bf16)
        q_cross[...] = join(cmulc(rec, g) if is_upper else cmulc(x, rec)).astype(bf16)

    pl.when(upper == 0)(functools.partial(run, False))
    pl.when(upper != 0)(functools.partial(run, True))
    filt_part(core, table, [(0, [(q_cross, 0), (q_near, half)]), (half, [(q_cross, half)])], gkeep, gsend)


def final_kernel(quarter, idx, q, k, g, own, far, own1, far1, r2, r3, mine, other, dq, dk, dv, grad_filt, held, filt_held, sems):
    z, upper, core = idx[0], idx[2], idx[3] & 1
    is_up = jnp.where(upper == 0, 0.0, 1.0)
    size = mine.shape[0]
    for which, piece in ((core, mine), (1 - core, other)):
        filt_held[pl.ds(pl.multiple_of(which * size, 8), size), :] = piece[...].astype(f32)
    copies = [pltpu.make_async_copy(filt_held, grad_filt, sems.at[3 * ROW_CHUNKS])]
    copies[0].start()
    rows = q.shape[1] // ROW_CHUNKS
    for c in range(ROW_CHUNKS):
        part = pl.ds(c * rows, rows)
        for r, src in enumerate((own, own1, far, far1)):
            cols = lanes((z ^ r) * quarter, quarter)
            conv = src[0, part].astype(f32)
            back = src[1, part].astype(f32)
            if r >= 2:
                add = (r2 if r == 2 else r3)[part].astype(f32)
                conv = conv + is_up * add
                back = back + (1.0 - is_up) * add
            held[0, part, cols] = (back * k[0, part, cols].astype(f32)).astype(bf16)
            held[1, part, cols] = (back * q[0, part, cols].astype(f32)).astype(bf16)
            held[2, part, cols] = (g[0, part, cols].astype(f32) * conv).astype(bf16)
        for j, dest in enumerate((dq, dk, dv)):
            copies.append(pltpu.make_async_copy(held.at[j, part], dest.at[0, part], sems.at[3 * c + j]))
            copies[-1].start()
    for copy in copies:
        copy.wait()


def half_plan(query_proj, key_proj, value_proj, out_grad, filter_taps):
    z = lax.axis_index("ctx").astype(jnp.int32)
    dp = lax.axis_index("dp").astype(jnp.int32)
    idx = jnp.stack([z, z & 1, z >> 1, dp])
    block, group = query_proj.shape[1:]
    quarter, length = filter_taps.shape
    half = length // 2
    rows = quarter // 2
    table = as_const(dft_table(length))
    macs = length * half * quarter

    def xz(vals, k):
        return lax.ppermute(vals, "ctx", [(i, i ^ k) for i in range(4)])

    def xd(vals, k):
        return lax.ppermute(vals, "dp", [(i, i ^ k) for i in range(4)])

    def apart(run, *args):
        shapes = jax.eval_shape(run, *args)
        return lax.cond(dp >= 0, run, lambda *_: jax.tree.map(lambda s: jnp.zeros(s.shape, s.dtype), shapes), *args)

    def over_cores(keep, send):
        return (keep + xd(send, 1).astype(f32)).astype(bf16)

    share = quarter // 4
    one, two, spec = ((block, quarter), bf16), ((2, block, quarter), bf16), ((length, quarter), bf16)
    act_in = ((1, block, group), lambda i, idx: (0, 0, 0))
    two_out = ((2, block, quarter), lambda i, idx: (0, 0, 0)) + two
    one_out = ((block, quarter), lambda i, idx: (0, 0)) + one
    gate_ins = [act_in] * 4 + [((share, half), lambda i, idx: (idx[3], 0))]
    gate_outs = [two_out] * 4 + [one_out] * 2 + [((share, half), lambda i, idx: (0, 0), (share, half), bf16)]
    keep_own, keep_far, own1, far1, to2, to3, piece = pl.pallas_call(
        functools.partial(gate_kernel, quarter),
        out_shape=[jax.ShapeDtypeStruct(s, d) for _, _, s, d in gate_outs],
        grid_spec=pltpu.PrefetchScalarGridSpec(
            num_scalar_prefetch=1,
            grid=(1,),
            in_specs=[pl.BlockSpec(blk, at) for blk, at in gate_ins],
            out_specs=[pl.BlockSpec(blk, at) for blk, at, _, _ in gate_outs],
        ),
        compiler_params=pltpu.CompilerParams(vmem_limit_bytes=GATE_VMEM),
        cost_estimate=pl.CostEstimate(flops=2 * block * group, bytes_accessed=16 * block * group, transcendentals=0),
    )(idx, query_proj, key_proj, value_proj, out_grad, filter_taps)
    near, cross, inv = call(
        own_filter_kernel, [spec] * 2 + [((half, length), bf16)], 2, smem_first=False, cost=(6 * macs, 16 * length * quarter)
    )(table, filter_taps)
    near, cross, inv, piece = lax.optimization_barrier((near, cross, inv, xz(piece, 2)))
    pair = jnp.concatenate([piece, xd(piece, 1)], 0)
    across = xd(pair, 2)
    far1, to2, to3, own1 = xz(far1, 1), xz(to2, 2), xz(to3, 3), xz(own1, 1)

    okeep_far, ofar1, *far_parts = call(
        conv_far_kernel,
        [two, two, ((rows, half), f32), ((rows, half), bf16)],
        6,
        cost=(32 * macs, 32 * length * quarter),
        limit=CONV_VMEM,
        scratch=[pltpu.VMEM((length, quarter), f32), pltpu.VMEM((length, quarter), bf16), pltpu.VMEM((4, half, quarter), bf16)],
    )(idx, table, inv, pair, across, keep_far, far1)
    ofar1 = xz(ofar1, 1)
    far = xz(apart(over_cores, *far_parts), 2)
    okeep, o1, o2, o3, *own_parts = call(
        conv_own_kernel,
        [two] * 2 + [one] * 2 + [((rows, length), f32), ((rows, length), bf16)],
        8,
        cost=(32 * macs, 32 * length * quarter),
        limit=CONV_VMEM,
        scratch=[pltpu.VMEM((length, quarter), bf16)] * 2 + [pltpu.VMEM((6, half, quarter), bf16)],
    )(idx, table, inv, near, cross, keep_own, own1, to2, to3)
    chip = apart(over_cores, *own_parts)

    def across_chips(chip, far, o1, o2, o3):
        chip = chip.astype(f32)
        chip = jnp.concatenate([chip[:, :half] + far.astype(f32), chip[:, half:]], 1)
        chip = lax.reduce_precision(chip, 8, 7).astype(bf16)
        theirs = xd(chip, 2)
        o1, o2, o3 = xz(o1, 1), xz(o2, 2), xz(o3, 3)

        def both_cores(chip, theirs):
            mine = (chip.astype(f32) + theirs.astype(f32)).astype(bf16)
            return mine, xd(mine, 1)

        return o1, o2, o3, *apart(both_cores, chip, theirs)

    o1, o2, o3, mine, other = apart(across_chips, chip, far, o1, o2, o3)
    act = (query_proj.shape, bf16)
    return call(
        functools.partial(final_kernel, quarter),
        [act] * 3 + [(filter_taps.shape, f32)],
        11,
        out_hbm=True,
        cost=(3 * block * group, 18 * block * group),
        scratch=[
            pltpu.VMEM((3, block, group), bf16),
            pltpu.VMEM(filter_taps.shape, f32),
            pltpu.SemaphoreType.DMA((3 * ROW_CHUNKS + 1,)),
        ],
    )(idx, query_proj, key_proj, out_grad, okeep, okeep_far, o1, ofar1, o2, o3, mine, other)


exact_mode = lax.Precision.HIGHEST
field_mode = lax.Precision.HIGH


def factor_sizes(length):
    col_count = min(128, length)
    return (2 * length // col_count, col_count)


def angle_table(first_size, second_size, period):
    product = (
        jnp.arange(first_size, dtype=jnp.int32)[:, None]
        * jnp.arange(second_size, dtype=jnp.int32)[None, :]
        % period
    )
    angles = product.astype(jnp.float32) * (2.0 * math.pi / period)
    return (jnp.cos(angles), jnp.sin(angles))


def make_tables(length):
    row_count, col_count = factor_sizes(length)
    outer_cos, outer_sin = angle_table(row_count, row_count // 2, row_count)
    twist_cos, twist_sin = angle_table(row_count, col_count, row_count * col_count)
    inner_cos, inner_sin = angle_table(col_count, col_count, col_count)
    real_outer = jnp.stack([outer_cos, -outer_sin])
    mixed_outer = jnp.stack([jnp.stack([outer_cos, outer_sin]), jnp.stack([-outer_sin, outer_cos])])
    fwd_twist = jnp.stack([twist_cos, -twist_sin])[:, None]
    inv_twist = jnp.stack([twist_cos, twist_sin])[:, None]
    fwd_inner = jnp.stack([jnp.stack([inner_cos, -inner_sin]), jnp.stack([inner_sin, inner_cos])])
    inv_inner = jnp.stack([jnp.stack([inner_cos, inner_sin]), jnp.stack([-inner_sin, inner_cos])])
    back_outer = jnp.stack([outer_cos, -outer_sin]) / float(row_count * col_count)
    return (real_outer, mixed_outer, fwd_twist, inv_twist, fwd_inner, inv_inner, back_outer)


def complex_mul(left, right):
    return jnp.stack(
        [left[0] * right[0] - left[1] * right[1], left[0] * right[1] + left[1] * right[0]]
    )


def conjugate(values):
    return jnp.stack([values[0], -values[1]])


def forward(values, tables, mode):
    real_outer, mixed_outer, fwd_twist, inv_twist, fwd_inner, inv_inner, back_outer = tables
    half_rows = real_outer.shape[2]
    col_count = fwd_inner.shape[2]
    grid = values.reshape(values.shape[0], half_rows, col_count)
    first = jnp.einsum("sca,hab->shcb", real_outer, grid, precision=mode)
    turned = complex_mul(first, fwd_twist)
    return jnp.einsum("shcb,stbd->thcd", turned, fwd_inner, precision=mode)


def inverse(spectrum, tables, mode):
    real_outer, mixed_outer, fwd_twist, inv_twist, fwd_inner, inv_inner, back_outer = tables
    back = jnp.einsum("shcd,stdb->thcb", spectrum, inv_inner, precision=mode)
    turned = complex_mul(back, inv_twist)
    out_grid = jnp.einsum("sca,shcb->hab", back_outer, turned, precision=mode)
    return out_grid.reshape(out_grid.shape[0], -1)


def whole_plan(query_proj, key_proj, value_proj, out_grad, filter_taps):
    query_vals = query_proj[0].astype(jnp.float32)
    key_vals = key_proj[0].astype(jnp.float32)
    grad_vals = out_grad[0].astype(jnp.float32)
    gated_vals = (query_vals * key_vals).astype(jnp.bfloat16).T
    grad_conv = (grad_vals * value_proj[0].astype(jnp.float32)).astype(jnp.bfloat16).T
    length = filter_taps.shape[1]
    tables = make_tables(length)
    filt_spec = forward(filter_taps, tables, exact_mode)
    gated_all = lax.all_to_all(gated_vals, "ctx", split_axis=0, concat_axis=1, tiled=True)
    gate_spec = forward(gated_all.astype(jnp.float32), tables, field_mode)
    conv_full = inverse(complex_mul(gate_spec, filt_spec), tables, field_mode).astype(jnp.bfloat16)
    conv_local = lax.all_to_all(conv_full, "ctx", split_axis=1, concat_axis=0, tiled=True)
    grad_all = lax.all_to_all(grad_conv, "ctx", split_axis=0, concat_axis=1, tiled=True)
    grad_spec = forward(grad_all.astype(jnp.float32), tables, field_mode)
    back_full = inverse(complex_mul(grad_spec, conjugate(filt_spec)), tables, field_mode).astype(
        jnp.bfloat16
    )
    back_local = lax.all_to_all(back_full, "ctx", split_axis=1, concat_axis=0, tiled=True)
    grad_v = (grad_vals * conv_local.T.astype(jnp.float32)).astype(jnp.bfloat16)[None]
    back_vals = back_local.T.astype(jnp.float32)
    grad_q = (back_vals * key_vals).astype(jnp.bfloat16)[None]
    grad_k = (back_vals * query_vals).astype(jnp.bfloat16)[None]
    cross_spec = complex_mul(conjugate(gate_spec), grad_spec)
    grad_filt = lax.psum(inverse(cross_spec, tables, exact_mode).astype(jnp.bfloat16), "dp").astype(
        jnp.float32
    )
    return (grad_q, grad_k, grad_v, grad_filt)

def solution(mesh):
    split = mesh.shape["ctx"] == 4 and mesh.shape["dp"] == 4
    body = half_plan if split else whole_plan
    acts = P("dp", "ctx", "chan")
    taps = P(("chan", "ctx"), None)
    return jax.shard_map(
        body,
        mesh=mesh,
        in_specs=(acts, acts, acts, acts, taps),
        out_specs=(acts, acts, acts, taps),
        check_vma=False,
    )
```

```python
import functools
import math

import jax
import jax.numpy as jnp
import ml_dtypes
import numpy as np
from jax import lax
from jax.experimental import pallas as pl
from jax.experimental.pallas import tpu as pltpu
from jax.sharding import PartitionSpec as P

bf16 = jnp.bfloat16
f32 = jnp.float32
VMEM_LIMIT = 20 * 1024 * 1024
CONV_VMEM = 20 * 1024 * 1024
GATE_VMEM = 63 * 1024 * 1024
ROW_CHUNKS = 4


def dft_table(size):
    freq = np.arange(size // 2)[:, None]
    pos = np.arange(-size // 2, size // 2)[None, :]
    angle = 2.0 * np.pi * (((2 * freq + 1) * pos) % (2 * size)) / (2 * size)
    return np.concatenate([np.cos(angle), -np.sin(angle)], 0)


def as_const(table):
    return jnp.asarray(np.ascontiguousarray(table).astype(ml_dtypes.bfloat16))


def mm(left, right, dims=((1,), (0,))):
    return lax.dot_general(left, right, (dims, ((), ())), preferred_element_type=f32)


def cmul(left, right):
    half = left.shape[0] // 2
    lr, li, rr, ri = left[:half], left[half:], right[:half], right[half:]
    return lr * rr - li * ri, lr * ri + li * rr


def cmulc(left, right):
    half = left.shape[0] // 2
    lr, li, rr, ri = left[:half], left[half:], right[:half], right[half:]
    return lr * rr + li * ri, lr * ri - li * rr


def join(pair):
    return jnp.concatenate([pair[0], pair[1]], 0)


def lanes(start, width):
    return pl.ds(pl.multiple_of(start, 128), width)


def call(kernel, outs, n_in, smem_first=True, cost=(0, 0), limit=VMEM_LIMIT, in_hbm=0, out_hbm=False, scratch=()):
    vmem, hbm = pl.BlockSpec(memory_space=pltpu.VMEM), pl.BlockSpec(memory_space=pl.ANY)
    in_specs = [hbm] * in_hbm + [vmem] * (n_in - in_hbm)
    if smem_first:
        in_specs = [pl.BlockSpec(memory_space=pltpu.SMEM)] + in_specs
    return pl.pallas_call(
        kernel,
        out_shape=[jax.ShapeDtypeStruct(s, d) for s, d in outs],
        in_specs=in_specs,
        out_specs=[hbm if out_hbm else vmem] * len(outs),
        scratch_shapes=scratch,
        compiler_params=pltpu.CompilerParams(vmem_limit_bytes=limit),
        cost_estimate=pl.CostEstimate(flops=cost[0], bytes_accessed=cost[1], transcendentals=0),
    )


def gate_kernel(quarter, idx, q, k, v, g, taps, keep_own, keep_far, own1, far1, to2, to3, piece):
    z, upper = idx[0], idx[2]
    piece[...] = taps[...].astype(bf16)
    for r, dest in ((3, far1), (2, keep_far), (1, own1), (0, keep_own)):
        cols = lanes((z ^ r) * quarter, quarter)
        gated = (q[0, :, cols].astype(f32) * k[0, :, cols].astype(f32)).astype(bf16)
        grad = (g[0, :, cols].astype(f32) * v[0, :, cols].astype(f32)).astype(bf16)
        dest[0] = gated
        dest[1] = grad
        if r >= 2:
            sel = jnp.where(upper == 0, gated.astype(f32), grad.astype(f32)).astype(bf16)
            (to2 if r == 2 else to3)[...] = sel


def own_filter_kernel(table, taps, near, cross, inv):
    half = taps.shape[1] // 2
    inv[...] = (table[:, half:].astype(f32).T * (1.0 / half)).astype(bf16)
    vals = taps[...].astype(bf16)
    cross[...] = mm(table[...], vals, ((1,), (1,))).astype(bf16)
    near[...] = mm(table[:, half:], vals[:, :half], ((1,), (1,))).astype(bf16)


def in_order(low, mine, partner, held):
    block = mine.shape[0]
    held[pl.ds(pl.multiple_of(low * block, block), block), :] = mine
    held[pl.ds(pl.multiple_of((1 - low) * block, block), block), :] = partner
    return held[...]


def halves(low, vals, held, mine, partner):
    held[...] = vals
    block = vals.shape[0] // 2
    mine[...] = held[pl.ds(pl.multiple_of(low * block, block), block), :]
    partner[...] = held[pl.ds(pl.multiple_of((1 - low) * block, block), block), :]


def filt_part(core, table, terms, keep, send):
    half = table.shape[1] // 2
    width = keep.shape[0]
    for dest, which in ((send, 1 - core), (keep, core)):
        cols = lanes(which * width, width)
        for first, pairs in terms:
            vals = sum(mm(q[:, cols], table[:, start : start + half], ((0,), (0,))) for q, start in pairs)
            dest[:, first : first + half] = (vals * (1.0 / half)).astype(dest.dtype)


def conv_far_kernel(idx, table, inv, mine, other, keep, recv, okeep, o1, gkeep, gsend, filt, q_far, held):
    low, core = idx[1], idx[3] & 1
    half = table.shape[1] // 2
    share = mine.shape[0]
    fwd = table[:, half:]
    x = mm(fwd, in_order(low, keep[0], recv[0], held.at[0]))
    g = mm(fwd, in_order(low, keep[1], recv[1], held.at[1]))
    for which, piece in ((core, mine), (1 - core, other)):
        filt[:, lanes(which * share, share)] = mm(fwd, piece[...], ((1,), (1,)))
    h = filt[...]
    q_far[...] = join(cmulc(x, g)).astype(bf16)
    for kind, pair in ((0, cmul(x, h)), (1, cmulc(h, g))):
        halves(low, mm(inv[...], join(pair).astype(bf16)).astype(bf16), held.at[2 + kind], okeep.at[kind], o1.at[kind])
    filt_part(core, table, [(0, [(q_far, half)])], gkeep, gsend)


def cross_kernel(idx, table, inv, cross, keep, recv, o2, o3, held):
    low, upper = idx[1], idx[2]
    half = table.shape[1] // 2
    spec = mm(table[:, half:], in_order(low, keep[upper], recv[upper], held.at[0]))
    h = cross[...].astype(f32)
    sign = jnp.where(upper == 0, 1.0, -1.0)
    pair = cmul(jnp.concatenate([h[:half], h[half:] * sign], 0), spec)
    halves(low, mm(inv[...], join(pair).astype(bf16)).astype(bf16), held.at[1], o2, o3)


def conv_own_kernel(idx, r2, r3, table, inv, near, cross, keep, recv, okeep, o1, gkeep, gsend, q_near, q_cross, held, sems):
    low, upper, core = idx[1], idx[2], idx[3] & 1
    half = table.shape[1] // 2
    block = r2.shape[0]
    loads = []
    for j, (src, place) in enumerate(((r2, low), (r3, 1 - low))):
        at = pl.ds(pl.multiple_of(place * block, block), block)
        loads.append(pltpu.make_async_copy(src, held.at[2, at], sems.at[j]))
        loads[j].start()

    def inverse(pair):
        return mm(inv[...], join(pair).astype(bf16)).astype(bf16)

    def run(is_upper):
        fwd = table[:, half:]
        x = mm(fwd, in_order(low, keep[0], recv[0], held.at[0]))
        g = mm(fwd, in_order(low, keep[1], recv[1], held.at[1]))
        for load in loads:
            load.wait()
        rec = mm(fwd, held[2])
        hx = cross[...].astype(f32)
        add = cmul(hx, rec) if is_upper else cmulc(hx, rec)
        h = near[...].astype(f32)
        conv = cmul(x, h)
        back = cmulc(h, g)
        if is_upper:
            conv = (conv[0] + add[0], conv[1] + add[1])
        else:
            back = (back[0] + add[0], back[1] + add[1])
        halves(low, inverse(conv), held.at[3], okeep.at[0], o1.at[0])
        halves(low, inverse(back), held.at[4], okeep.at[1], o1.at[1])
        q_near[...] = join(cmulc(x, g)).astype(bf16)
        q_cross[...] = join(cmulc(rec, g) if is_upper else cmulc(x, rec)).astype(bf16)

    pl.when(upper == 0)(functools.partial(run, False))
    pl.when(upper != 0)(functools.partial(run, True))
    filt_part(core, table, [(0, [(q_cross, 0), (q_near, half)]), (half, [(q_cross, half)])], gkeep, gsend)


def final_kernel(quarter, idx, q, k, g, own, far, own1, far1, r2, r3, mine, other, dq, dk, dv, grad_filt, held, filt_held, sems):
    z, upper, core = idx[0], idx[2], idx[3] & 1
    is_up = jnp.where(upper == 0, 0.0, 1.0)
    size = mine.shape[0]
    for which, piece in ((core, mine), (1 - core, other)):
        filt_held[pl.ds(pl.multiple_of(which * size, 8), size), :] = piece[...].astype(f32)
    copies = [pltpu.make_async_copy(filt_held, grad_filt, sems.at[3 * ROW_CHUNKS])]
    copies[0].start()
    rows = q.shape[1] // ROW_CHUNKS
    for c in range(ROW_CHUNKS):
        part = pl.ds(c * rows, rows)
        for r, src in enumerate((own, own1, far, far1)):
            cols = lanes((z ^ r) * quarter, quarter)
            conv = src[0, part].astype(f32)
            back = src[1, part].astype(f32)
            if r >= 2:
                add = (r2 if r == 2 else r3)[part].astype(f32)
                conv = conv + is_up * add
                back = back + (1.0 - is_up) * add
            held[0, part, cols] = (back * k[0, part, cols].astype(f32)).astype(bf16)
            held[1, part, cols] = (back * q[0, part, cols].astype(f32)).astype(bf16)
            held[2, part, cols] = (g[0, part, cols].astype(f32) * conv).astype(bf16)
        for j, dest in enumerate((dq, dk, dv)):
            copies.append(pltpu.make_async_copy(held.at[j, part], dest.at[0, part], sems.at[3 * c + j]))
            copies[-1].start()
    for copy in copies:
        copy.wait()


def half_plan(query_proj, key_proj, value_proj, out_grad, filter_taps):
    z = lax.axis_index("ctx").astype(jnp.int32)
    dp = lax.axis_index("dp").astype(jnp.int32)
    idx = jnp.stack([z, z & 1, z >> 1, dp])
    block, group = query_proj.shape[1:]
    quarter, length = filter_taps.shape
    half = length // 2
    rows = quarter // 2
    table = as_const(dft_table(length))
    macs = length * half * quarter

    def xz(vals, k):
        return lax.ppermute(vals, "ctx", [(i, i ^ k) for i in range(4)])

    def xd(vals, k):
        return lax.ppermute(vals, "dp", [(i, i ^ k) for i in range(4)])

    def apart(run, *args):
        shapes = jax.eval_shape(run, *args)
        return lax.cond(dp >= 0, run, lambda *_: jax.tree.map(lambda s: jnp.zeros(s.shape, s.dtype), shapes), *args)

    def over_cores(keep, send):
        return (keep.astype(f32) + xd(send, 1).astype(f32)).astype(bf16)

    share = quarter // 2
    one, two, spec = ((block, quarter), bf16), ((2, block, quarter), bf16), ((length, quarter), bf16)
    act_in = ((1, block, group), lambda i, idx: (0, 0, 0))
    two_out = ((2, block, quarter), lambda i, idx: (0, 0, 0)) + two
    one_out = ((block, quarter), lambda i, idx: (0, 0)) + one
    gate_ins = [act_in] * 4 + [((share, half), lambda i, idx: (idx[3] & 1, 0))]
    gate_outs = [two_out] * 4 + [one_out] * 2 + [((share, half), lambda i, idx: (0, 0), (share, half), bf16)]
    keep_own, keep_far, own1, far1, to2, to3, piece = pl.pallas_call(
        functools.partial(gate_kernel, quarter),
        out_shape=[jax.ShapeDtypeStruct(s, d) for _, _, s, d in gate_outs],
        grid_spec=pltpu.PrefetchScalarGridSpec(
            num_scalar_prefetch=1,
            grid=(1,),
            in_specs=[pl.BlockSpec(blk, at) for blk, at in gate_ins],
            out_specs=[pl.BlockSpec(blk, at) for blk, at, _, _ in gate_outs],
        ),
        compiler_params=pltpu.CompilerParams(vmem_limit_bytes=GATE_VMEM),
        cost_estimate=pl.CostEstimate(flops=2 * block * group, bytes_accessed=16 * block * group, transcendentals=0),
    )(idx, query_proj, key_proj, value_proj, out_grad, filter_taps)
    piece = xz(piece, 2)
    near, cross, inv = call(
        own_filter_kernel, [spec] * 2 + [((half, length), bf16)], 2, smem_first=False, cost=(6 * macs, 16 * length * quarter)
    )(table, filter_taps)
    near, cross, inv, piece = lax.optimization_barrier((near, cross, inv, piece))
    other_piece = xd(piece, 1)
    far1, to2, to3, own1 = xz(far1, 1), xz(to2, 2), xz(to3, 3), xz(own1, 1)
    okeep_far, ofar1, *far_parts = call(
        conv_far_kernel,
        [two] * 2 + [((rows, half), bf16)] * 2,
        6,
        cost=(8 * macs, 32 * length * quarter),
        limit=CONV_VMEM,
        scratch=[pltpu.VMEM((length, quarter), f32), pltpu.VMEM((length, quarter), bf16), pltpu.VMEM((4, half, quarter), bf16)],
    )(idx, table, inv, piece, other_piece, keep_far, far1)
    ofar1 = xz(ofar1, 1)
    far = apart(over_cores, *far_parts)
    far, cross = lax.optimization_barrier((far, cross))
    far = xz(far, 2)
    o2, o3 = call(
        cross_kernel, [one] * 2, 5, cost=(4 * macs, 8 * length * quarter), scratch=[pltpu.VMEM((2, half, quarter), bf16)]
    )(idx, table, inv, cross, keep_own, own1)
    o2, o3 = xz(o2, 2), xz(o3, 3)
    okeep, o1, *own_parts = call(
        conv_own_kernel,
        [two] * 2 + [((rows, length), bf16)] * 2,
        8,
        in_hbm=2,
        cost=(48 * macs, 32 * length * quarter),
        limit=CONV_VMEM,
        scratch=[pltpu.VMEM((length, quarter), bf16)] * 2
        + [pltpu.VMEM((5, half, quarter), bf16), pltpu.SemaphoreType.DMA((2,))],
    )(idx, to2, to3, table, inv, near, cross, keep_own, own1)
    chip = apart(over_cores, *own_parts)

    def across_chips(chip, far, o1):
        low = lax.reduce_precision(chip[:, :half].astype(f32) + far.astype(f32), 8, 7).astype(bf16)
        chip = jnp.concatenate([low, chip[:, half:]], 1)
        theirs = xd(chip, 2)
        o1 = xz(o1, 1)

        def both_cores(chip, theirs):
            mine = (chip.astype(f32) + theirs.astype(f32)).astype(bf16)
            return mine, xd(mine, 1)

        return o1, *apart(both_cores, chip, theirs)

    o1, mine, other = apart(across_chips, chip, far, o1)
    act = (query_proj.shape, bf16)
    return call(
        functools.partial(final_kernel, quarter),
        [act] * 3 + [(filter_taps.shape, f32)],
        11,
        out_hbm=True,
        cost=(3 * block * group, 18 * block * group),
        scratch=[
            pltpu.VMEM((3, block, group), bf16),
            pltpu.VMEM(filter_taps.shape, f32),
            pltpu.SemaphoreType.DMA((3 * ROW_CHUNKS + 1,)),
        ],
    )(idx, query_proj, key_proj, out_grad, okeep, okeep_far, o1, ofar1, o2, o3, mine, other)


exact_mode = lax.Precision.HIGHEST
field_mode = lax.Precision.HIGH


def factor_sizes(length):
    col_count = min(128, length)
    return (2 * length // col_count, col_count)


def angle_table(first_size, second_size, period):
    product = (
        jnp.arange(first_size, dtype=jnp.int32)[:, None]
        * jnp.arange(second_size, dtype=jnp.int32)[None, :]
        % period
    )
    angles = product.astype(jnp.float32) * (2.0 * math.pi / period)
    return (jnp.cos(angles), jnp.sin(angles))


def make_tables(length):
    row_count, col_count = factor_sizes(length)
    outer_cos, outer_sin = angle_table(row_count, row_count // 2, row_count)
    twist_cos, twist_sin = angle_table(row_count, col_count, row_count * col_count)
    inner_cos, inner_sin = angle_table(col_count, col_count, col_count)
    real_outer = jnp.stack([outer_cos, -outer_sin])
    mixed_outer = jnp.stack([jnp.stack([outer_cos, outer_sin]), jnp.stack([-outer_sin, outer_cos])])
    fwd_twist = jnp.stack([twist_cos, -twist_sin])[:, None]
    inv_twist = jnp.stack([twist_cos, twist_sin])[:, None]
    fwd_inner = jnp.stack([jnp.stack([inner_cos, -inner_sin]), jnp.stack([inner_sin, inner_cos])])
    inv_inner = jnp.stack([jnp.stack([inner_cos, inner_sin]), jnp.stack([-inner_sin, inner_cos])])
    back_outer = jnp.stack([outer_cos, -outer_sin]) / float(row_count * col_count)
    return (real_outer, mixed_outer, fwd_twist, inv_twist, fwd_inner, inv_inner, back_outer)


def complex_mul(left, right):
    return jnp.stack(
        [left[0] * right[0] - left[1] * right[1], left[0] * right[1] + left[1] * right[0]]
    )


def conjugate(values):
    return jnp.stack([values[0], -values[1]])


def forward(values, tables, mode):
    real_outer, mixed_outer, fwd_twist, inv_twist, fwd_inner, inv_inner, back_outer = tables
    half_rows = real_outer.shape[2]
    col_count = fwd_inner.shape[2]
    grid = values.reshape(values.shape[0], half_rows, col_count)
    first = jnp.einsum("sca,hab->shcb", real_outer, grid, precision=mode)
    turned = complex_mul(first, fwd_twist)
    return jnp.einsum("shcb,stbd->thcd", turned, fwd_inner, precision=mode)


def inverse(spectrum, tables, mode):
    real_outer, mixed_outer, fwd_twist, inv_twist, fwd_inner, inv_inner, back_outer = tables
    back = jnp.einsum("shcd,stdb->thcb", spectrum, inv_inner, precision=mode)
    turned = complex_mul(back, inv_twist)
    out_grid = jnp.einsum("sca,shcb->hab", back_outer, turned, precision=mode)
    return out_grid.reshape(out_grid.shape[0], -1)


def whole_plan(query_proj, key_proj, value_proj, out_grad, filter_taps):
    query_vals = query_proj[0].astype(jnp.float32)
    key_vals = key_proj[0].astype(jnp.float32)
    grad_vals = out_grad[0].astype(jnp.float32)
    gated_vals = (query_vals * key_vals).astype(jnp.bfloat16).T
    grad_conv = (grad_vals * value_proj[0].astype(jnp.float32)).astype(jnp.bfloat16).T
    length = filter_taps.shape[1]
    tables = make_tables(length)
    filt_spec = forward(filter_taps, tables, exact_mode)
    gated_all = lax.all_to_all(gated_vals, "ctx", split_axis=0, concat_axis=1, tiled=True)
    gate_spec = forward(gated_all.astype(jnp.float32), tables, field_mode)
    conv_full = inverse(complex_mul(gate_spec, filt_spec), tables, field_mode).astype(jnp.bfloat16)
    conv_local = lax.all_to_all(conv_full, "ctx", split_axis=1, concat_axis=0, tiled=True)
    grad_all = lax.all_to_all(grad_conv, "ctx", split_axis=0, concat_axis=1, tiled=True)
    grad_spec = forward(grad_all.astype(jnp.float32), tables, field_mode)
    back_full = inverse(complex_mul(grad_spec, conjugate(filt_spec)), tables, field_mode).astype(
        jnp.bfloat16
    )
    back_local = lax.all_to_all(back_full, "ctx", split_axis=1, concat_axis=0, tiled=True)
    grad_v = (grad_vals * conv_local.T.astype(jnp.float32)).astype(jnp.bfloat16)[None]
    back_vals = back_local.T.astype(jnp.float32)
    grad_q = (back_vals * key_vals).astype(jnp.bfloat16)[None]
    grad_k = (back_vals * query_vals).astype(jnp.bfloat16)[None]
    cross_spec = complex_mul(conjugate(gate_spec), grad_spec)
    grad_filt = lax.psum(inverse(cross_spec, tables, exact_mode).astype(jnp.bfloat16), "dp").astype(
        jnp.float32
    )
    return (grad_q, grad_k, grad_v, grad_filt)

def solution(mesh):
    split = mesh.shape["ctx"] == 4 and mesh.shape["dp"] == 4
    body = half_plan if split else whole_plan
    acts = P("dp", "ctx", "chan")
    taps = P(("chan", "ctx"), None)
    return jax.shard_map(
        body,
        mesh=mesh,
        in_specs=(acts, acts, acts, acts, taps),
        out_specs=(acts, acts, acts, taps),
        check_vma=False,
    )
```

```python
import functools
import math

import jax
import jax.numpy as jnp
import ml_dtypes
import numpy as np
from jax import lax
from jax.experimental import pallas as pl
from jax.experimental.pallas import tpu as pltpu
from jax.sharding import PartitionSpec as P

bf16 = jnp.bfloat16
f32 = jnp.float32
VMEM_LIMIT = 20 * 1024 * 1024
CONV_VMEM = 20 * 1024 * 1024
GATE_VMEM = 63 * 1024 * 1024
ROW_CHUNKS = 4


def dft_table(size):
    freq = np.arange(size // 2)[:, None]
    pos = np.arange(-size // 2, size // 2)[None, :]
    angle = 2.0 * np.pi * (((2 * freq + 1) * pos) % (2 * size)) / (2 * size)
    return np.concatenate([np.cos(angle), -np.sin(angle)], 0)


def as_const(table):
    return jnp.asarray(np.ascontiguousarray(table).astype(ml_dtypes.bfloat16))


def mm(left, right, dims=((1,), (0,))):
    return lax.dot_general(left, right, (dims, ((), ())), preferred_element_type=f32)


def cmul(left, right):
    half = left.shape[0] // 2
    lr, li, rr, ri = left[:half], left[half:], right[:half], right[half:]
    return lr * rr - li * ri, lr * ri + li * rr


def cmulc(left, right):
    half = left.shape[0] // 2
    lr, li, rr, ri = left[:half], left[half:], right[:half], right[half:]
    return lr * rr + li * ri, lr * ri - li * rr


def join(pair):
    return jnp.concatenate([pair[0], pair[1]], 0)


def lanes(start, width):
    return pl.ds(pl.multiple_of(start, 128), width)


def call(kernel, outs, n_in, smem_first=True, cost=(0, 0), limit=VMEM_LIMIT, in_hbm=0, out_hbm=False, scratch=()):
    vmem, hbm = pl.BlockSpec(memory_space=pltpu.VMEM), pl.BlockSpec(memory_space=pl.ANY)
    in_specs = [hbm] * in_hbm + [vmem] * (n_in - in_hbm)
    if smem_first:
        in_specs = [pl.BlockSpec(memory_space=pltpu.SMEM)] + in_specs
    return pl.pallas_call(
        kernel,
        out_shape=[jax.ShapeDtypeStruct(s, d) for s, d in outs],
        in_specs=in_specs,
        out_specs=[hbm if out_hbm else vmem] * len(outs),
        scratch_shapes=scratch,
        compiler_params=pltpu.CompilerParams(vmem_limit_bytes=limit),
        cost_estimate=pl.CostEstimate(flops=cost[0], bytes_accessed=cost[1], transcendentals=0),
    )


def gate_kernel(quarter, idx, q, k, v, g, taps, keep_own, keep_far, own1, far1, to2, to3, piece):
    z, upper = idx[0], idx[2]
    piece[...] = taps[...].astype(bf16)
    for r, dest in ((3, far1), (2, keep_far), (1, own1), (0, keep_own)):
        cols = lanes((z ^ r) * quarter, quarter)
        gated = (q[0, :, cols].astype(f32) * k[0, :, cols].astype(f32)).astype(bf16)
        grad = (g[0, :, cols].astype(f32) * v[0, :, cols].astype(f32)).astype(bf16)
        dest[0] = gated
        dest[1] = grad
        if r >= 2:
            sel = jnp.where(upper == 0, gated.astype(f32), grad.astype(f32)).astype(bf16)
            (to2 if r == 2 else to3)[...] = sel


def own_filter_kernel(table, taps, near, cross, inv):
    half = taps.shape[1] // 2
    inv[...] = (table[:, half:].astype(f32).T * (1.0 / half)).astype(bf16)
    vals = taps[...].astype(bf16)
    cross[...] = mm(table[...], vals, ((1,), (1,))).astype(bf16)
    near[...] = mm(table[:, half:], vals[:, :half], ((1,), (1,))).astype(bf16)


def in_order(low, mine, partner, held):
    block = mine.shape[0]
    held[pl.ds(pl.multiple_of(low * block, block), block), :] = mine
    held[pl.ds(pl.multiple_of((1 - low) * block, block), block), :] = partner
    return held[...]


def halves(low, vals, held, mine, partner):
    held[...] = vals
    block = vals.shape[0] // 2
    mine[...] = held[pl.ds(pl.multiple_of(low * block, block), block), :]
    partner[...] = held[pl.ds(pl.multiple_of((1 - low) * block, block), block), :]


def filt_part(core, table, terms, keep, send):
    half = table.shape[1] // 2
    width = keep.shape[0]
    for dest, which in ((send, 1 - core), (keep, core)):
        cols = lanes(which * width, width)
        for first, pairs in terms:
            vals = sum(mm(q[:, cols], table[:, start : start + half], ((0,), (0,))) for q, start in pairs)
            dest[:, first : first + half] = (vals * (1.0 / half)).astype(dest.dtype)


def conv_far_kernel(idx, table, inv, mine, other, keep, recv, okeep, o1, gkeep, gsend, filt, q_far, held):
    low, core = idx[1], idx[3] & 1
    half = table.shape[1] // 2
    share = mine.shape[0]
    fwd = table[:, half:]
    x = mm(fwd, in_order(low, keep[0], recv[0], held.at[0]))
    g = mm(fwd, in_order(low, keep[1], recv[1], held.at[1]))
    for which, piece in ((core, mine), (1 - core, other)):
        filt[:, lanes(which * share, share)] = mm(fwd, piece[...], ((1,), (1,)))
    h = filt[...]
    q_far[...] = join(cmulc(x, g)).astype(bf16)
    for kind, pair in ((0, cmul(x, h)), (1, cmulc(h, g))):
        halves(low, mm(inv[...], join(pair).astype(bf16)).astype(bf16), held.at[2 + kind], okeep.at[kind], o1.at[kind])
    filt_part(core, table, [(0, [(q_far, half)])], gkeep, gsend)


def cross_kernel(idx, table, inv, cross, keep, recv, o2, o3, held):
    low, upper = idx[1], idx[2]
    half = table.shape[1] // 2
    spec = mm(table[:, half:], in_order(low, keep[upper], recv[upper], held.at[0]))
    h = cross[...].astype(f32)
    sign = jnp.where(upper == 0, 1.0, -1.0)
    pair = cmul(jnp.concatenate([h[:half], h[half:] * sign], 0), spec)
    halves(low, mm(inv[...], join(pair).astype(bf16)).astype(bf16), held.at[1], o2, o3)


def load_blocks(low, r2, r3, held, sems):
    block = r2.shape[0]
    loads = []
    for j, (src, place) in enumerate(((r2, low), (r3, 1 - low))):
        at = pl.ds(pl.multiple_of(place * block, block), block)
        loads.append(pltpu.make_async_copy(src, held.at[at], sems.at[j]))
        loads[j].start()
    return loads


def own_filter_grad_kernel(idx, r2, r3, table, keep, recv, gkeep, gsend, q_near, q_cross, held, sems):
    low, upper, core = idx[1], idx[2], idx[3] & 1
    half = table.shape[1] // 2
    loads = load_blocks(low, r2, r3, held.at[2], sems)
    fwd = table[:, half:]
    x = mm(fwd, in_order(low, keep[0], recv[0], held.at[0]))
    g = mm(fwd, in_order(low, keep[1], recv[1], held.at[1]))
    q_near[...] = join(cmulc(x, g)).astype(bf16)
    for load in loads:
        load.wait()
    rec = mm(fwd, held[2])

    def lower():
        q_cross[...] = join(cmulc(x, rec)).astype(bf16)

    def higher():
        q_cross[...] = join(cmulc(rec, g)).astype(bf16)

    pl.when(upper == 0)(lower)
    pl.when(upper != 0)(higher)
    filt_part(core, table, [(0, [(q_cross, 0), (q_near, half)]), (half, [(q_cross, half)])], gkeep, gsend)


def conv_own_kernel(idx, r2, r3, table, inv, near, cross, keep, recv, okeep, o1, held, sems):
    low, upper = idx[1], idx[2]
    half = table.shape[1] // 2
    loads = load_blocks(low, r2, r3, held.at[2], sems)
    fwd = table[:, half:]
    x = mm(fwd, in_order(low, keep[0], recv[0], held.at[0]))
    g = mm(fwd, in_order(low, keep[1], recv[1], held.at[1]))
    h = near[...].astype(f32)
    hx = cross[...].astype(f32)
    for load in loads:
        load.wait()
    rec = mm(fwd, held[2])

    def put(kind, pair):
        vals = mm(inv[...], join(pair).astype(bf16)).astype(bf16)
        halves(low, vals, held.at[3 + kind], okeep.at[kind], o1.at[kind])

    def lower():
        put(0, cmul(x, h))
        back, add = cmulc(h, g), cmulc(hx, rec)
        put(1, (back[0] + add[0], back[1] + add[1]))

    def higher():
        conv, add = cmul(x, h), cmul(hx, rec)
        put(0, (conv[0] + add[0], conv[1] + add[1]))
        put(1, cmulc(h, g))

    pl.when(upper == 0)(lower)
    pl.when(upper != 0)(higher)


def final_kernel(quarter, idx, q, k, g, own, far, own1, far1, r2, r3, mine, other, dq, dk, dv, grad_filt, held, filt_held, sems):
    z, upper, core = idx[0], idx[2], idx[3] & 1
    is_up = jnp.where(upper == 0, 0.0, 1.0)
    size = mine.shape[0]
    for which, piece in ((core, mine), (1 - core, other)):
        filt_held[pl.ds(pl.multiple_of(which * size, 8), size), :] = piece[...].astype(f32)
    copies = [pltpu.make_async_copy(filt_held, grad_filt, sems.at[3 * ROW_CHUNKS])]
    copies[0].start()
    rows = q.shape[1] // ROW_CHUNKS
    for c in range(ROW_CHUNKS):
        part = pl.ds(c * rows, rows)
        for r, src in enumerate((own, own1, far, far1)):
            cols = lanes((z ^ r) * quarter, quarter)
            conv = src[0, part].astype(f32)
            back = src[1, part].astype(f32)
            if r >= 2:
                add = (r2 if r == 2 else r3)[part].astype(f32)
                conv = conv + is_up * add
                back = back + (1.0 - is_up) * add
            held[0, part, cols] = (back * k[0, part, cols].astype(f32)).astype(bf16)
            held[1, part, cols] = (back * q[0, part, cols].astype(f32)).astype(bf16)
            held[2, part, cols] = (g[0, part, cols].astype(f32) * conv).astype(bf16)
        for j, dest in enumerate((dq, dk, dv)):
            copies.append(pltpu.make_async_copy(held.at[j, part], dest.at[0, part], sems.at[3 * c + j]))
            copies[-1].start()
    for copy in copies:
        copy.wait()


def half_plan(query_proj, key_proj, value_proj, out_grad, filter_taps):
    z = lax.axis_index("ctx").astype(jnp.int32)
    dp = lax.axis_index("dp").astype(jnp.int32)
    idx = jnp.stack([z, z & 1, z >> 1, dp])
    block, group = query_proj.shape[1:]
    quarter, length = filter_taps.shape
    half = length // 2
    rows = quarter // 2
    table = as_const(dft_table(length))
    macs = length * half * quarter

    def xz(vals, k):
        return lax.ppermute(vals, "ctx", [(i, i ^ k) for i in range(4)])

    def xd(vals, k):
        return lax.ppermute(vals, "dp", [(i, i ^ k) for i in range(4)])

    def apart(run, *args):
        shapes = jax.eval_shape(run, *args)
        return lax.cond(dp >= 0, run, lambda *_: jax.tree.map(lambda s: jnp.zeros(s.shape, s.dtype), shapes), *args)

    def over_cores(keep, send):
        return (keep.astype(f32) + xd(send, 1).astype(f32)).astype(bf16)

    share = quarter // 2
    one, two, spec = ((block, quarter), bf16), ((2, block, quarter), bf16), ((length, quarter), bf16)
    act_in = ((1, block, group), lambda i, idx: (0, 0, 0))
    two_out = ((2, block, quarter), lambda i, idx: (0, 0, 0)) + two
    one_out = ((block, quarter), lambda i, idx: (0, 0)) + one
    gate_ins = [act_in] * 4 + [((share, half), lambda i, idx: (idx[3] & 1, 0))]
    gate_outs = [two_out] * 4 + [one_out] * 2 + [((share, half), lambda i, idx: (0, 0), (share, half), bf16)]
    keep_own, keep_far, own1, far1, to2, to3, piece = pl.pallas_call(
        functools.partial(gate_kernel, quarter),
        out_shape=[jax.ShapeDtypeStruct(s, d) for _, _, s, d in gate_outs],
        grid_spec=pltpu.PrefetchScalarGridSpec(
            num_scalar_prefetch=1,
            grid=(1,),
            in_specs=[pl.BlockSpec(blk, at) for blk, at in gate_ins],
            out_specs=[pl.BlockSpec(blk, at) for blk, at, _, _ in gate_outs],
        ),
        compiler_params=pltpu.CompilerParams(vmem_limit_bytes=GATE_VMEM),
        cost_estimate=pl.CostEstimate(flops=2 * block * group, bytes_accessed=16 * block * group, transcendentals=0),
    )(idx, query_proj, key_proj, value_proj, out_grad, filter_taps)
    piece = xz(piece, 2)
    near, cross, inv = call(
        own_filter_kernel, [spec] * 2 + [((half, length), bf16)], 2, smem_first=False, cost=(6 * macs, 16 * length * quarter)
    )(table, filter_taps)
    near, cross, inv, piece = lax.optimization_barrier((near, cross, inv, piece))
    other_piece = xd(piece, 1)
    far1, to2, to3, own1 = xz(far1, 1), xz(to2, 2), xz(to3, 3), xz(own1, 1)
    okeep_far, ofar1, *far_parts = call(
        conv_far_kernel,
        [two] * 2 + [((rows, half), bf16)] * 2,
        6,
        cost=(8 * macs, 32 * length * quarter),
        limit=CONV_VMEM,
        scratch=[pltpu.VMEM((length, quarter), f32), pltpu.VMEM((length, quarter), bf16), pltpu.VMEM((4, half, quarter), bf16)],
    )(idx, table, inv, piece, other_piece, keep_far, far1)
    ofar1 = xz(ofar1, 1)
    far = apart(over_cores, *far_parts)
    far, cross = lax.optimization_barrier((far, cross))
    far = xz(far, 2)
    o2, o3 = call(
        cross_kernel, [one] * 2, 5, cost=(4 * macs, 8 * length * quarter), scratch=[pltpu.VMEM((2, half, quarter), bf16)]
    )(idx, table, inv, cross, keep_own, own1)
    o2, o3 = xz(o2, 2), xz(o3, 3)
    own_parts = call(
        own_filter_grad_kernel,
        [((rows, length), bf16)] * 2,
        5,
        in_hbm=2,
        cost=(48 * macs, 32 * length * quarter),
        limit=CONV_VMEM,
        scratch=[pltpu.VMEM((length, quarter), bf16)] * 2
        + [pltpu.VMEM((3, half, quarter), bf16), pltpu.SemaphoreType.DMA((2,))],
    )(idx, to2, to3, table, keep_own, own1)

    def own_quarter(own_parts, far, idx, *conv_ins):
        chip = own_parts[0].astype(f32) + xd(own_parts[1], 1).astype(f32)
        chip = jnp.concatenate([chip[:, :half] + far.astype(f32), chip[:, half:]], 1)
        chip = lax.reduce_precision(chip, 8, 7).astype(bf16)
        theirs = xd(chip, 2)
        okeep, o1 = call(
            conv_own_kernel,
            [two] * 2,
            8,
            in_hbm=2,
            cost=(4 * macs, 4 * length * quarter),
            limit=CONV_VMEM,
            scratch=[pltpu.VMEM((5, half, quarter), bf16), pltpu.SemaphoreType.DMA((2,))],
        )(idx, *conv_ins)
        o1 = xz(o1, 1)

        def both_cores(chip, theirs):
            mine = (chip.astype(f32) + theirs.astype(f32)).astype(bf16)
            return mine, xd(mine, 1)

        return okeep, o1, *apart(both_cores, chip, theirs)

    okeep, o1, mine, other = apart(
        own_quarter, own_parts, far, idx, to2, to3, table, inv, near, cross, keep_own, own1
    )
    act = (query_proj.shape, bf16)
    return call(
        functools.partial(final_kernel, quarter),
        [act] * 3 + [(filter_taps.shape, f32)],
        11,
        out_hbm=True,
        cost=(3 * block * group, 18 * block * group),
        scratch=[
            pltpu.VMEM((3, block, group), bf16),
            pltpu.VMEM(filter_taps.shape, f32),
            pltpu.SemaphoreType.DMA((3 * ROW_CHUNKS + 1,)),
        ],
    )(idx, query_proj, key_proj, out_grad, okeep, okeep_far, o1, ofar1, o2, o3, mine, other)


exact_mode = lax.Precision.HIGHEST
field_mode = lax.Precision.HIGH


def factor_sizes(length):
    col_count = min(128, length)
    return (2 * length // col_count, col_count)


def angle_table(first_size, second_size, period):
    product = (
        jnp.arange(first_size, dtype=jnp.int32)[:, None]
        * jnp.arange(second_size, dtype=jnp.int32)[None, :]
        % period
    )
    angles = product.astype(jnp.float32) * (2.0 * math.pi / period)
    return (jnp.cos(angles), jnp.sin(angles))


def make_tables(length):
    row_count, col_count = factor_sizes(length)
    outer_cos, outer_sin = angle_table(row_count, row_count // 2, row_count)
    twist_cos, twist_sin = angle_table(row_count, col_count, row_count * col_count)
    inner_cos, inner_sin = angle_table(col_count, col_count, col_count)
    real_outer = jnp.stack([outer_cos, -outer_sin])
    mixed_outer = jnp.stack([jnp.stack([outer_cos, outer_sin]), jnp.stack([-outer_sin, outer_cos])])
    fwd_twist = jnp.stack([twist_cos, -twist_sin])[:, None]
    inv_twist = jnp.stack([twist_cos, twist_sin])[:, None]
    fwd_inner = jnp.stack([jnp.stack([inner_cos, -inner_sin]), jnp.stack([inner_sin, inner_cos])])
    inv_inner = jnp.stack([jnp.stack([inner_cos, inner_sin]), jnp.stack([-inner_sin, inner_cos])])
    back_outer = jnp.stack([outer_cos, -outer_sin]) / float(row_count * col_count)
    return (real_outer, mixed_outer, fwd_twist, inv_twist, fwd_inner, inv_inner, back_outer)


def complex_mul(left, right):
    return jnp.stack(
        [left[0] * right[0] - left[1] * right[1], left[0] * right[1] + left[1] * right[0]]
    )


def conjugate(values):
    return jnp.stack([values[0], -values[1]])


def forward(values, tables, mode):
    real_outer, mixed_outer, fwd_twist, inv_twist, fwd_inner, inv_inner, back_outer = tables
    half_rows = real_outer.shape[2]
    col_count = fwd_inner.shape[2]
    grid = values.reshape(values.shape[0], half_rows, col_count)
    first = jnp.einsum("sca,hab->shcb", real_outer, grid, precision=mode)
    turned = complex_mul(first, fwd_twist)
    return jnp.einsum("shcb,stbd->thcd", turned, fwd_inner, precision=mode)


def inverse(spectrum, tables, mode):
    real_outer, mixed_outer, fwd_twist, inv_twist, fwd_inner, inv_inner, back_outer = tables
    back = jnp.einsum("shcd,stdb->thcb", spectrum, inv_inner, precision=mode)
    turned = complex_mul(back, inv_twist)
    out_grid = jnp.einsum("sca,shcb->hab", back_outer, turned, precision=mode)
    return out_grid.reshape(out_grid.shape[0], -1)


def whole_plan(query_proj, key_proj, value_proj, out_grad, filter_taps):
    query_vals = query_proj[0].astype(jnp.float32)
    key_vals = key_proj[0].astype(jnp.float32)
    grad_vals = out_grad[0].astype(jnp.float32)
    gated_vals = (query_vals * key_vals).astype(jnp.bfloat16).T
    grad_conv = (grad_vals * value_proj[0].astype(jnp.float32)).astype(jnp.bfloat16).T
    length = filter_taps.shape[1]
    tables = make_tables(length)
    filt_spec = forward(filter_taps, tables, exact_mode)
    gated_all = lax.all_to_all(gated_vals, "ctx", split_axis=0, concat_axis=1, tiled=True)
    gate_spec = forward(gated_all.astype(jnp.float32), tables, field_mode)
    conv_full = inverse(complex_mul(gate_spec, filt_spec), tables, field_mode).astype(jnp.bfloat16)
    conv_local = lax.all_to_all(conv_full, "ctx", split_axis=1, concat_axis=0, tiled=True)
    grad_all = lax.all_to_all(grad_conv, "ctx", split_axis=0, concat_axis=1, tiled=True)
    grad_spec = forward(grad_all.astype(jnp.float32), tables, field_mode)
    back_full = inverse(complex_mul(grad_spec, conjugate(filt_spec)), tables, field_mode).astype(
        jnp.bfloat16
    )
    back_local = lax.all_to_all(back_full, "ctx", split_axis=1, concat_axis=0, tiled=True)
    grad_v = (grad_vals * conv_local.T.astype(jnp.float32)).astype(jnp.bfloat16)[None]
    back_vals = back_local.T.astype(jnp.float32)
    grad_q = (back_vals * key_vals).astype(jnp.bfloat16)[None]
    grad_k = (back_vals * query_vals).astype(jnp.bfloat16)[None]
    cross_spec = complex_mul(conjugate(gate_spec), grad_spec)
    grad_filt = lax.psum(inverse(cross_spec, tables, exact_mode).astype(jnp.bfloat16), "dp").astype(
        jnp.float32
    )
    return (grad_q, grad_k, grad_v, grad_filt)

def solution(mesh):
    split = mesh.shape["ctx"] == 4 and mesh.shape["dp"] == 4
    body = half_plan if split else whole_plan
    acts = P("dp", "ctx", "chan")
    taps = P(("chan", "ctx"), None)
    return jax.shard_map(
        body,
        mesh=mesh,
        in_specs=(acts, acts, acts, acts, taps),
        out_specs=(acts, acts, acts, taps),
        check_vma=False,
    )
```

```python
import functools
import math

import jax
import jax.numpy as jnp
import ml_dtypes
import numpy as np
from jax import lax
from jax.experimental import pallas as pl
from jax.experimental.pallas import tpu as pltpu
from jax.sharding import PartitionSpec as P

bf16 = jnp.bfloat16
f32 = jnp.float32
VMEM_LIMIT = 20 * 1024 * 1024
CONV_VMEM = 20 * 1024 * 1024
GATE_VMEM = 63 * 1024 * 1024
ROW_CHUNKS = 4


def dft_table(size):
    freq = np.arange(size // 2)[:, None]
    pos = np.arange(-size // 2, size // 2)[None, :]
    angle = 2.0 * np.pi * (((2 * freq + 1) * pos) % (2 * size)) / (2 * size)
    return np.concatenate([np.cos(angle), -np.sin(angle)], 0)


def as_const(table):
    return jnp.asarray(np.ascontiguousarray(table).astype(ml_dtypes.bfloat16))


def mm(left, right, dims=((1,), (0,))):
    return lax.dot_general(left, right, (dims, ((), ())), preferred_element_type=f32)


def cmul(left, right):
    half = left.shape[0] // 2
    lr, li, rr, ri = left[:half], left[half:], right[:half], right[half:]
    return lr * rr - li * ri, lr * ri + li * rr


def cmulc(left, right):
    half = left.shape[0] // 2
    lr, li, rr, ri = left[:half], left[half:], right[:half], right[half:]
    return lr * rr + li * ri, lr * ri - li * rr


def join(pair):
    return jnp.concatenate([pair[0], pair[1]], 0)


def lanes(start, width):
    return pl.ds(pl.multiple_of(start, 128), width)


def call(kernel, outs, n_in, smem_first=True, cost=(0, 0), limit=VMEM_LIMIT, in_hbm=0, out_hbm=False, scratch=()):
    vmem, hbm = pl.BlockSpec(memory_space=pltpu.VMEM), pl.BlockSpec(memory_space=pl.ANY)
    in_specs = [hbm] * in_hbm + [vmem] * (n_in - in_hbm)
    if smem_first:
        in_specs = [pl.BlockSpec(memory_space=pltpu.SMEM)] + in_specs
    return pl.pallas_call(
        kernel,
        out_shape=[jax.ShapeDtypeStruct(s, d) for s, d in outs],
        in_specs=in_specs,
        out_specs=[hbm if out_hbm else vmem] * len(outs),
        scratch_shapes=scratch,
        compiler_params=pltpu.CompilerParams(vmem_limit_bytes=limit),
        cost_estimate=pl.CostEstimate(flops=cost[0], bytes_accessed=cost[1], transcendentals=0),
    )


def gate_kernel(quarter, idx, q, k, v, g, taps, keep_own, keep_far, own1, far1, to2, to3, piece):
    z, upper = idx[0], idx[2]
    piece[...] = taps[...].astype(bf16)
    for r, dest in ((3, far1), (2, keep_far), (1, own1), (0, keep_own)):
        cols = lanes((z ^ r) * quarter, quarter)
        gated = (q[0, :, cols].astype(f32) * k[0, :, cols].astype(f32)).astype(bf16)
        grad = (g[0, :, cols].astype(f32) * v[0, :, cols].astype(f32)).astype(bf16)
        dest[0] = gated
        dest[1] = grad
        if r >= 2:
            sel = jnp.where(upper == 0, gated.astype(f32), grad.astype(f32)).astype(bf16)
            (to2 if r == 2 else to3)[...] = sel


def own_filter_kernel(table, taps, near, cross, inv):
    half = taps.shape[1] // 2
    inv[...] = (table[:, half:].astype(f32).T * (1.0 / half)).astype(bf16)
    vals = taps[...].astype(bf16)
    cross[...] = mm(table[...], vals, ((1,), (1,))).astype(bf16)
    near[...] = mm(table[:, half:], vals[:, :half], ((1,), (1,))).astype(bf16)


def in_order(low, mine, partner, held):
    block = mine.shape[0]
    held[pl.ds(pl.multiple_of(low * block, block), block), :] = mine
    held[pl.ds(pl.multiple_of((1 - low) * block, block), block), :] = partner
    return held[...]


def halves(low, vals, held, mine, partner):
    held[...] = vals
    block = vals.shape[0] // 2
    mine[...] = held[pl.ds(pl.multiple_of(low * block, block), block), :]
    partner[...] = held[pl.ds(pl.multiple_of((1 - low) * block, block), block), :]


def filt_part(core, table, terms, keep, send):
    half = table.shape[1] // 2
    width = keep.shape[0]
    for dest, which in ((send, 1 - core), (keep, core)):
        cols = lanes(which * width, width)
        for first, pairs in terms:
            vals = sum(mm(q[:, cols], table[:, start : start + half], ((0,), (0,))) for q, start in pairs)
            dest[:, first : first + half] = (vals * (1.0 / half)).astype(dest.dtype)


def conv_far_kernel(idx, table, inv, mine, other, keep, recv, okeep, o1, gkeep, gsend, filt, q_far, held):
    low, core = idx[1], idx[3] & 1
    half = table.shape[1] // 2
    share = mine.shape[0]
    fwd = table[:, half:]
    x = mm(fwd, in_order(low, keep[0], recv[0], held.at[0]))
    g = mm(fwd, in_order(low, keep[1], recv[1], held.at[1]))
    for which, piece in ((core, mine), (1 - core, other)):
        filt[:, lanes(which * share, share)] = mm(fwd, piece[...], ((1,), (1,)))
    h = filt[...]
    q_far[...] = join(cmulc(x, g)).astype(bf16)
    for kind, pair in ((0, cmul(x, h)), (1, cmulc(h, g))):
        halves(low, mm(inv[...], join(pair).astype(bf16)).astype(bf16), held.at[2 + kind], okeep.at[kind], o1.at[kind])
    filt_part(core, table, [(0, [(q_far, half)])], gkeep, gsend)


def cross_kernel(idx, table, inv, cross, keep, recv, o2, o3, held):
    low, upper = idx[1], idx[2]
    half = table.shape[1] // 2
    spec = mm(table[:, half:], in_order(low, keep[upper], recv[upper], held.at[0]))
    h = cross[...].astype(f32)
    sign = jnp.where(upper == 0, 1.0, -1.0)
    pair = cmul(jnp.concatenate([h[:half], h[half:] * sign], 0), spec)
    halves(low, mm(inv[...], join(pair).astype(bf16)).astype(bf16), held.at[1], o2, o3)


def load_blocks(low, r2, r3, held, sems):
    block = r2.shape[0]
    loads = []
    for j, (src, place) in enumerate(((r2, low), (r3, 1 - low))):
        at = pl.ds(pl.multiple_of(place * block, block), block)
        loads.append(pltpu.make_async_copy(src, held.at[at], sems.at[j]))
        loads[j].start()
    return loads


def own_filter_grad_kernel(idx, r2, r3, table, keep, recv, gkeep, gsend, q_near, q_cross, held, sems):
    low, upper, core = idx[1], idx[2], idx[3] & 1
    half = table.shape[1] // 2
    loads = load_blocks(low, r2, r3, held.at[2], sems)
    fwd = table[:, half:]
    x = mm(fwd, in_order(low, keep[0], recv[0], held.at[0]))
    g = mm(fwd, in_order(low, keep[1], recv[1], held.at[1]))
    q_near[...] = join(cmulc(x, g)).astype(bf16)
    for load in loads:
        load.wait()
    rec = mm(fwd, held[2])

    def lower():
        q_cross[...] = join(cmulc(x, rec)).astype(bf16)

    def higher():
        q_cross[...] = join(cmulc(rec, g)).astype(bf16)

    pl.when(upper == 0)(lower)
    pl.when(upper != 0)(higher)
    filt_part(core, table, [(0, [(q_cross, 0), (q_near, half)]), (half, [(q_cross, half)])], gkeep, gsend)


def conv_own_kernel(idx, r2, r3, table, inv, near, cross, keep, recv, okeep, o1, held, sems):
    low, upper = idx[1], idx[2]
    half = table.shape[1] // 2
    loads = load_blocks(low, r2, r3, held.at[2], sems)
    fwd = table[:, half:]
    x = mm(fwd, in_order(low, keep[0], recv[0], held.at[0]))
    g = mm(fwd, in_order(low, keep[1], recv[1], held.at[1]))
    h = near[...].astype(f32)
    hx = cross[...].astype(f32)
    for load in loads:
        load.wait()
    rec = mm(fwd, held[2])

    def put(kind, pair):
        vals = mm(inv[...], join(pair).astype(bf16)).astype(bf16)
        halves(low, vals, held.at[3 + kind], okeep.at[kind], o1.at[kind])

    def lower():
        put(0, cmul(x, h))
        back, add = cmulc(h, g), cmulc(hx, rec)
        put(1, (back[0] + add[0], back[1] + add[1]))

    def higher():
        conv, add = cmul(x, h), cmul(hx, rec)
        put(0, (conv[0] + add[0], conv[1] + add[1]))
        put(1, cmulc(h, g))

    pl.when(upper == 0)(lower)
    pl.when(upper != 0)(higher)


def final_kernel(quarter, idx, q, k, g, own, far, own1, far1, r2, r3, mine, other, dq, dk, dv, grad_filt, held, filt_held, sems):
    z, upper, core = idx[0], idx[2], idx[3] & 1
    is_up = jnp.where(upper == 0, 0.0, 1.0)
    size = mine.shape[0]
    for which, piece in ((core, mine), (1 - core, other)):
        filt_held[pl.ds(pl.multiple_of(which * size, 8), size), :] = piece[...].astype(f32)
    copies = [pltpu.make_async_copy(filt_held, grad_filt, sems.at[3 * ROW_CHUNKS])]
    copies[0].start()
    rows = q.shape[1] // ROW_CHUNKS
    for c in range(ROW_CHUNKS):
        part = pl.ds(c * rows, rows)
        for r, src in enumerate((own, own1, far, far1)):
            cols = lanes((z ^ r) * quarter, quarter)
            conv = src[0, part].astype(f32)
            back = src[1, part].astype(f32)
            if r >= 2:
                add = (r2 if r == 2 else r3)[part].astype(f32)
                conv = conv + is_up * add
                back = back + (1.0 - is_up) * add
            held[0, part, cols] = (back * k[0, part, cols].astype(f32)).astype(bf16)
            held[1, part, cols] = (back * q[0, part, cols].astype(f32)).astype(bf16)
            held[2, part, cols] = (g[0, part, cols].astype(f32) * conv).astype(bf16)
        for j, dest in enumerate((dq, dk, dv)):
            copies.append(pltpu.make_async_copy(held.at[j, part], dest.at[0, part], sems.at[3 * c + j]))
            copies[-1].start()
    for copy in copies:
        copy.wait()


def half_plan(query_proj, key_proj, value_proj, out_grad, filter_taps):
    z = lax.axis_index("ctx").astype(jnp.int32)
    dp = lax.axis_index("dp").astype(jnp.int32)
    idx = jnp.stack([z, z & 1, z >> 1, dp])
    block, group = query_proj.shape[1:]
    quarter, length = filter_taps.shape
    half = length // 2
    rows = quarter // 2
    table = as_const(dft_table(length))
    macs = length * half * quarter

    def xz(vals, k):
        return lax.ppermute(vals, "ctx", [(i, i ^ k) for i in range(4)])

    def xd(vals, k):
        return lax.ppermute(vals, "dp", [(i, i ^ k) for i in range(4)])

    def apart(run, *args):
        shapes = jax.eval_shape(run, *args)
        return lax.cond(dp >= 0, run, lambda *_: jax.tree.map(lambda s: jnp.zeros(s.shape, s.dtype), shapes), *args)

    def over_cores(keep, send):
        return (keep.astype(f32) + xd(send, 1).astype(f32)).astype(bf16)

    share = quarter // 2
    one, two, spec = ((block, quarter), bf16), ((2, block, quarter), bf16), ((length, quarter), bf16)
    act_in = ((1, block, group), lambda i, idx: (0, 0, 0))
    two_out = ((2, block, quarter), lambda i, idx: (0, 0, 0)) + two
    one_out = ((block, quarter), lambda i, idx: (0, 0)) + one
    gate_ins = [act_in] * 4 + [((share, half), lambda i, idx: (idx[3] & 1, 0))]
    gate_outs = [two_out] * 4 + [one_out] * 2 + [((share, half), lambda i, idx: (0, 0), (share, half), bf16)]
    keep_own, keep_far, own1, far1, to2, to3, piece = pl.pallas_call(
        functools.partial(gate_kernel, quarter),
        out_shape=[jax.ShapeDtypeStruct(s, d) for _, _, s, d in gate_outs],
        grid_spec=pltpu.PrefetchScalarGridSpec(
            num_scalar_prefetch=1,
            grid=(1,),
            in_specs=[pl.BlockSpec(blk, at) for blk, at in gate_ins],
            out_specs=[pl.BlockSpec(blk, at) for blk, at, _, _ in gate_outs],
        ),
        compiler_params=pltpu.CompilerParams(vmem_limit_bytes=GATE_VMEM),
        cost_estimate=pl.CostEstimate(flops=2 * block * group, bytes_accessed=16 * block * group, transcendentals=0),
    )(idx, query_proj, key_proj, value_proj, out_grad, filter_taps)
    piece = xz(piece, 2)
    near, cross, inv = call(
        own_filter_kernel, [spec] * 2 + [((half, length), bf16)], 2, smem_first=False, cost=(6 * macs, 16 * length * quarter)
    )(table, filter_taps)
    near, cross, inv, piece = lax.optimization_barrier((near, cross, inv, piece))
    other_piece = xd(piece, 1)
    far1, to2, to3, own1 = xz(far1, 1), xz(to2, 2), xz(to3, 3), xz(own1, 1)

    def far_quarter(idx, inv, piece, other_piece, keep_far, far1):
        okeep, o1, *parts = call(
            conv_far_kernel,
            [two] * 2 + [((rows, half), bf16)] * 2,
            6,
            cost=(8 * macs, 32 * length * quarter),
            limit=CONV_VMEM,
            scratch=[pltpu.VMEM((length, quarter), f32), pltpu.VMEM((length, quarter), bf16), pltpu.VMEM((4, half, quarter), bf16)],
        )(idx, table, inv, piece, other_piece, keep_far, far1)
        return okeep, o1, over_cores(*parts)

    okeep_far, ofar1, far = apart(far_quarter, idx, inv, piece, other_piece, keep_far, far1)
    ofar1 = xz(ofar1, 1)
    far, cross = lax.optimization_barrier((far, cross))
    far = xz(far, 2)
    o2, o3 = call(
        cross_kernel, [one] * 2, 5, cost=(4 * macs, 8 * length * quarter), scratch=[pltpu.VMEM((2, half, quarter), bf16)]
    )(idx, table, inv, cross, keep_own, own1)
    o2, o3 = xz(o2, 2), xz(o3, 3)
    own_parts = call(
        own_filter_grad_kernel,
        [((rows, length), bf16)] * 2,
        5,
        in_hbm=2,
        cost=(48 * macs, 32 * length * quarter),
        limit=CONV_VMEM,
        scratch=[pltpu.VMEM((length, quarter), bf16)] * 2
        + [pltpu.VMEM((3, half, quarter), bf16), pltpu.SemaphoreType.DMA((2,))],
    )(idx, to2, to3, table, keep_own, own1)

    def own_quarter(own_parts, far, idx, *conv_ins):
        chip = own_parts[0].astype(f32) + xd(own_parts[1], 1).astype(f32)
        chip = jnp.concatenate([chip[:, :half] + far.astype(f32), chip[:, half:]], 1)
        chip = lax.reduce_precision(chip, 8, 7).astype(bf16)
        theirs = xd(chip, 2)
        okeep, o1 = call(
            conv_own_kernel,
            [two] * 2,
            8,
            in_hbm=2,
            cost=(4 * macs, 4 * length * quarter),
            limit=CONV_VMEM,
            scratch=[pltpu.VMEM((5, half, quarter), bf16), pltpu.SemaphoreType.DMA((2,))],
        )(idx, *conv_ins)
        o1 = xz(o1, 1)

        def both_cores(chip, theirs):
            mine = (chip.astype(f32) + theirs.astype(f32)).astype(bf16)
            return mine, xd(mine, 1)

        return okeep, o1, *apart(both_cores, chip, theirs)

    okeep, o1, mine, other = apart(
        own_quarter, own_parts, far, idx, to2, to3, table, inv, near, cross, keep_own, own1
    )
    act = (query_proj.shape, bf16)
    return call(
        functools.partial(final_kernel, quarter),
        [act] * 3 + [(filter_taps.shape, f32)],
        11,
        out_hbm=True,
        cost=(3 * block * group, 18 * block * group),
        scratch=[
            pltpu.VMEM((3, block, group), bf16),
            pltpu.VMEM(filter_taps.shape, f32),
            pltpu.SemaphoreType.DMA((3 * ROW_CHUNKS + 1,)),
        ],
    )(idx, query_proj, key_proj, out_grad, okeep, okeep_far, o1, ofar1, o2, o3, mine, other)


exact_mode = lax.Precision.HIGHEST
field_mode = lax.Precision.HIGH


def factor_sizes(length):
    col_count = min(128, length)
    return (2 * length // col_count, col_count)


def angle_table(first_size, second_size, period):
    product = (
        jnp.arange(first_size, dtype=jnp.int32)[:, None]
        * jnp.arange(second_size, dtype=jnp.int32)[None, :]
        % period
    )
    angles = product.astype(jnp.float32) * (2.0 * math.pi / period)
    return (jnp.cos(angles), jnp.sin(angles))


def make_tables(length):
    row_count, col_count = factor_sizes(length)
    outer_cos, outer_sin = angle_table(row_count, row_count // 2, row_count)
    twist_cos, twist_sin = angle_table(row_count, col_count, row_count * col_count)
    inner_cos, inner_sin = angle_table(col_count, col_count, col_count)
    real_outer = jnp.stack([outer_cos, -outer_sin])
    mixed_outer = jnp.stack([jnp.stack([outer_cos, outer_sin]), jnp.stack([-outer_sin, outer_cos])])
    fwd_twist = jnp.stack([twist_cos, -twist_sin])[:, None]
    inv_twist = jnp.stack([twist_cos, twist_sin])[:, None]
    fwd_inner = jnp.stack([jnp.stack([inner_cos, -inner_sin]), jnp.stack([inner_sin, inner_cos])])
    inv_inner = jnp.stack([jnp.stack([inner_cos, inner_sin]), jnp.stack([-inner_sin, inner_cos])])
    back_outer = jnp.stack([outer_cos, -outer_sin]) / float(row_count * col_count)
    return (real_outer, mixed_outer, fwd_twist, inv_twist, fwd_inner, inv_inner, back_outer)


def complex_mul(left, right):
    return jnp.stack(
        [left[0] * right[0] - left[1] * right[1], left[0] * right[1] + left[1] * right[0]]
    )


def conjugate(values):
    return jnp.stack([values[0], -values[1]])


def forward(values, tables, mode):
    real_outer, mixed_outer, fwd_twist, inv_twist, fwd_inner, inv_inner, back_outer = tables
    half_rows = real_outer.shape[2]
    col_count = fwd_inner.shape[2]
    grid = values.reshape(values.shape[0], half_rows, col_count)
    first = jnp.einsum("sca,hab->shcb", real_outer, grid, precision=mode)
    turned = complex_mul(first, fwd_twist)
    return jnp.einsum("shcb,stbd->thcd", turned, fwd_inner, precision=mode)


def inverse(spectrum, tables, mode):
    real_outer, mixed_outer, fwd_twist, inv_twist, fwd_inner, inv_inner, back_outer = tables
    back = jnp.einsum("shcd,stdb->thcb", spectrum, inv_inner, precision=mode)
    turned = complex_mul(back, inv_twist)
    out_grid = jnp.einsum("sca,shcb->hab", back_outer, turned, precision=mode)
    return out_grid.reshape(out_grid.shape[0], -1)


def whole_plan(query_proj, key_proj, value_proj, out_grad, filter_taps):
    query_vals = query_proj[0].astype(jnp.float32)
    key_vals = key_proj[0].astype(jnp.float32)
    grad_vals = out_grad[0].astype(jnp.float32)
    gated_vals = (query_vals * key_vals).astype(jnp.bfloat16).T
    grad_conv = (grad_vals * value_proj[0].astype(jnp.float32)).astype(jnp.bfloat16).T
    length = filter_taps.shape[1]
    tables = make_tables(length)
    filt_spec = forward(filter_taps, tables, exact_mode)
    gated_all = lax.all_to_all(gated_vals, "ctx", split_axis=0, concat_axis=1, tiled=True)
    gate_spec = forward(gated_all.astype(jnp.float32), tables, field_mode)
    conv_full = inverse(complex_mul(gate_spec, filt_spec), tables, field_mode).astype(jnp.bfloat16)
    conv_local = lax.all_to_all(conv_full, "ctx", split_axis=1, concat_axis=0, tiled=True)
    grad_all = lax.all_to_all(grad_conv, "ctx", split_axis=0, concat_axis=1, tiled=True)
    grad_spec = forward(grad_all.astype(jnp.float32), tables, field_mode)
    back_full = inverse(complex_mul(grad_spec, conjugate(filt_spec)), tables, field_mode).astype(
        jnp.bfloat16
    )
    back_local = lax.all_to_all(back_full, "ctx", split_axis=1, concat_axis=0, tiled=True)
    grad_v = (grad_vals * conv_local.T.astype(jnp.float32)).astype(jnp.bfloat16)[None]
    back_vals = back_local.T.astype(jnp.float32)
    grad_q = (back_vals * key_vals).astype(jnp.bfloat16)[None]
    grad_k = (back_vals * query_vals).astype(jnp.bfloat16)[None]
    cross_spec = complex_mul(conjugate(gate_spec), grad_spec)
    grad_filt = lax.psum(inverse(cross_spec, tables, exact_mode).astype(jnp.bfloat16), "dp").astype(
        jnp.float32
    )
    return (grad_q, grad_k, grad_v, grad_filt)

def solution(mesh):
    split = mesh.shape["ctx"] == 4 and mesh.shape["dp"] == 4
    body = half_plan if split else whole_plan
    acts = P("dp", "ctx", "chan")
    taps = P(("chan", "ctx"), None)
    return jax.shard_map(
        body,
        mesh=mesh,
        in_specs=(acts, acts, acts, acts, taps),
        out_specs=(acts, acts, acts, taps),
        check_vma=False,
    )
```

```python
import functools
import math

import jax
import jax.numpy as jnp
import ml_dtypes
import numpy as np
from jax import lax
from jax.experimental import pallas as pl
from jax.experimental.pallas import tpu as pltpu
from jax.sharding import PartitionSpec as P

bf16 = jnp.bfloat16
f32 = jnp.float32
VMEM_LIMIT = 20 * 1024 * 1024
CONV_VMEM = 20 * 1024 * 1024
GATE_VMEM = 58 * 1024 * 1024
ROW_CHUNKS = 2
FILT_CHUNKS = 4


def dft_table(size):
    freq = np.arange(size // 2)[:, None]
    pos = np.arange(-size // 2, size // 2)[None, :]
    angle = 2.0 * np.pi * (((2 * freq + 1) * pos) % (2 * size)) / (2 * size)
    return np.concatenate([np.cos(angle), -np.sin(angle)], 0)


def as_const(table):
    return jnp.asarray(np.ascontiguousarray(table).astype(ml_dtypes.bfloat16))


def mm(left, right, dims=((1,), (0,))):
    return lax.dot_general(left, right, (dims, ((), ())), preferred_element_type=f32)


def cmul(left, right):
    half = left.shape[0] // 2
    lr, li, rr, ri = left[:half], left[half:], right[:half], right[half:]
    return lr * rr - li * ri, lr * ri + li * rr


def cmulc(left, right):
    half = left.shape[0] // 2
    lr, li, rr, ri = left[:half], left[half:], right[:half], right[half:]
    return lr * rr + li * ri, lr * ri - li * rr


def join(pair):
    return jnp.concatenate([pair[0], pair[1]], 0)


def lanes(start, width):
    return pl.ds(pl.multiple_of(start, 128), width)


def call(kernel, outs, n_in, smem_first=True, cost=(0, 0), limit=VMEM_LIMIT, in_hbm=0, out_hbm=False, scratch=()):
    vmem, hbm = pl.BlockSpec(memory_space=pltpu.VMEM), pl.BlockSpec(memory_space=pl.ANY)
    in_specs = [hbm] * in_hbm + [vmem] * (n_in - in_hbm)
    if smem_first:
        in_specs = [pl.BlockSpec(memory_space=pltpu.SMEM)] + in_specs
    return pl.pallas_call(
        kernel,
        out_shape=[jax.ShapeDtypeStruct(s, d) for s, d in outs],
        in_specs=in_specs,
        out_specs=[hbm if out_hbm else vmem] * len(outs),
        scratch_shapes=scratch,
        compiler_params=pltpu.CompilerParams(vmem_limit_bytes=limit),
        cost_estimate=pl.CostEstimate(flops=cost[0], bytes_accessed=cost[1], transcendentals=0),
    )


def gate_kernel(quarter, idx, q, k, v, g, taps, keep_own, keep_far, own1, far1, to2, to3, piece):
    z, upper = idx[0], idx[2]
    piece[...] = taps[...].astype(bf16)
    for r, dest in ((3, far1), (2, keep_far), (1, own1), (0, keep_own)):
        cols = lanes((z ^ r) * quarter, quarter)
        gated = (q[0, :, cols].astype(f32) * k[0, :, cols].astype(f32)).astype(bf16)
        grad = (g[0, :, cols].astype(f32) * v[0, :, cols].astype(f32)).astype(bf16)
        dest[0] = gated
        dest[1] = grad
        if r >= 2:
            sel = jnp.where(upper == 0, gated.astype(f32), grad.astype(f32)).astype(bf16)
            (to2 if r == 2 else to3)[...] = sel


def own_filter_kernel(table, taps, near, cross, inv):
    half = taps.shape[1] // 2
    inv[...] = (table[:, half:].astype(f32).T * (1.0 / half)).astype(bf16)
    vals = taps[...].astype(bf16)
    cross[...] = mm(table[...], vals, ((1,), (1,))).astype(bf16)
    near[...] = mm(table[:, half:], vals[:, :half], ((1,), (1,))).astype(bf16)


def in_order(low, mine, partner, held):
    block = mine.shape[0]
    held[pl.ds(pl.multiple_of(low * block, block), block), :] = mine
    held[pl.ds(pl.multiple_of((1 - low) * block, block), block), :] = partner
    return held[...]


def halves(low, vals, held, mine, partner):
    held[...] = vals
    block = vals.shape[0] // 2
    mine[...] = held[pl.ds(pl.multiple_of(low * block, block), block), :]
    partner[...] = held[pl.ds(pl.multiple_of((1 - low) * block, block), block), :]


def filt_part(core, table, terms, keep, send):
    half = table.shape[1] // 2
    width = keep.shape[0]
    for dest, which in ((send, 1 - core), (keep, core)):
        cols = lanes(which * width, width)
        for first, pairs in terms:
            vals = sum(mm(q[:, cols], table[:, start : start + half], ((0,), (0,))) for q, start in pairs)
            dest[:, first : first + half] = (vals * (1.0 / half)).astype(dest.dtype)


def conv_far_kernel(idx, table, inv, mine, other, keep, recv, okeep, o1, gkeep, gsend, filt, q_far, held):
    low, core = idx[1], idx[3] & 1
    half = table.shape[1] // 2
    share = mine.shape[0]
    fwd = table[:, half:]
    x = mm(fwd, in_order(low, keep[0], recv[0], held.at[0]))
    g = mm(fwd, in_order(low, keep[1], recv[1], held.at[1]))
    for which, piece in ((core, mine), (1 - core, other)):
        filt[:, lanes(which * share, share)] = mm(fwd, piece[...], ((1,), (1,)))
    h = filt[...]
    q_far[...] = join(cmulc(x, g)).astype(bf16)
    for kind, pair in ((0, cmul(x, h)), (1, cmulc(h, g))):
        halves(low, mm(inv[...], join(pair).astype(bf16)).astype(bf16), held.at[2 + kind], okeep.at[kind], o1.at[kind])
    filt_part(core, table, [(0, [(q_far, half)])], gkeep, gsend)


def cross_kernel(idx, table, inv, cross, keep, recv, o2, o3, held):
    low, upper = idx[1], idx[2]
    half = table.shape[1] // 2
    spec = mm(table[:, half:], in_order(low, keep[upper], recv[upper], held.at[0]))
    h = cross[...].astype(f32)
    sign = jnp.where(upper == 0, 1.0, -1.0)
    pair = cmul(jnp.concatenate([h[:half], h[half:] * sign], 0), spec)
    halves(low, mm(inv[...], join(pair).astype(bf16)).astype(bf16), held.at[1], o2, o3)


def load_blocks(low, r2, r3, held, sems):
    block = r2.shape[0]
    loads = []
    for j, (src, place) in enumerate(((r2, low), (r3, 1 - low))):
        at = pl.ds(pl.multiple_of(place * block, block), block)
        loads.append(pltpu.make_async_copy(src, held.at[at], sems.at[j]))
        loads[j].start()
    return loads


def own_filter_grad_kernel(idx, r2, r3, table, keep, recv, gkeep, gsend, q_near, q_cross, held, sems):
    low, upper, core = idx[1], idx[2], idx[3] & 1
    half = table.shape[1] // 2
    loads = load_blocks(low, r2, r3, held.at[2], sems)
    fwd = table[:, half:]
    x = mm(fwd, in_order(low, keep[0], recv[0], held.at[0]))
    g = mm(fwd, in_order(low, keep[1], recv[1], held.at[1]))
    q_near[...] = join(cmulc(x, g)).astype(bf16)
    for load in loads:
        load.wait()
    rec = mm(fwd, held[2])

    def lower():
        q_cross[...] = join(cmulc(x, rec)).astype(bf16)

    def higher():
        q_cross[...] = join(cmulc(rec, g)).astype(bf16)

    pl.when(upper == 0)(lower)
    pl.when(upper != 0)(higher)
    filt_part(core, table, [(0, [(q_cross, 0), (q_near, half)]), (half, [(q_cross, half)])], gkeep, gsend)


def conv_own_kernel(idx, r2, r3, table, inv, near, cross, keep, recv, okeep, o1, held, sems):
    low, upper = idx[1], idx[2]
    half = table.shape[1] // 2
    loads = load_blocks(low, r2, r3, held.at[2], sems)
    fwd = table[:, half:]
    x = mm(fwd, in_order(low, keep[0], recv[0], held.at[0]))
    g = mm(fwd, in_order(low, keep[1], recv[1], held.at[1]))
    h = near[...].astype(f32)
    hx = cross[...].astype(f32)
    for load in loads:
        load.wait()
    rec = mm(fwd, held[2])

    def put(kind, pair):
        vals = mm(inv[...], join(pair).astype(bf16)).astype(bf16)
        halves(low, vals, held.at[3 + kind], okeep.at[kind], o1.at[kind])

    def lower():
        put(0, cmul(x, h))
        back, add = cmulc(h, g), cmulc(hx, rec)
        put(1, (back[0] + add[0], back[1] + add[1]))

    def higher():
        conv, add = cmul(x, h), cmul(hx, rec)
        put(0, (conv[0] + add[0], conv[1] + add[1]))
        put(1, cmulc(h, g))

    pl.when(upper == 0)(lower)
    pl.when(upper != 0)(higher)


def final_kernel(quarter, idx, q, k, g, own, far, own1, far1, r2, r3, mine, other, dq, dk, dv, grad_filt, held, filt_held, sems):
    z, upper, core = idx[0], idx[2], idx[3] & 1
    is_up = jnp.where(upper == 0, 0.0, 1.0)
    size = mine.shape[0]
    part_size = size // FILT_CHUNKS
    copies = []
    for which, piece in ((core, mine), (1 - core, other)):
        for j in range(FILT_CHUNKS):
            at = pl.ds(pl.multiple_of(which * size + j * part_size, 8), part_size)
            filt_held[at, :] = piece[j * part_size : (j + 1) * part_size, :].astype(f32)
            copies.append(pltpu.make_async_copy(filt_held.at[at], grad_filt.at[at], sems.at[3 * ROW_CHUNKS + len(copies)]))
            copies[-1].start()
    rows = q.shape[1] // ROW_CHUNKS
    for c in range(ROW_CHUNKS):
        part = pl.ds(c * rows, rows)
        for r, src in enumerate((own, own1, far, far1)):
            cols = lanes((z ^ r) * quarter, quarter)
            conv = src[0, part].astype(f32)
            back = src[1, part].astype(f32)
            if r >= 2:
                add = (r2 if r == 2 else r3)[part].astype(f32)
                conv = conv + is_up * add
                back = back + (1.0 - is_up) * add
            held[0, part, cols] = (back * k[0, part, cols].astype(f32)).astype(bf16)
            held[1, part, cols] = (back * q[0, part, cols].astype(f32)).astype(bf16)
            held[2, part, cols] = (g[0, part, cols].astype(f32) * conv).astype(bf16)
        for j, dest in enumerate((dq, dk, dv)):
            copies.append(pltpu.make_async_copy(held.at[j, part], dest.at[0, part], sems.at[3 * c + j]))
            copies[-1].start()
    for copy in copies:
        copy.wait()


def half_plan(query_proj, key_proj, value_proj, out_grad, filter_taps):
    z = lax.axis_index("ctx").astype(jnp.int32)
    dp = lax.axis_index("dp").astype(jnp.int32)
    idx = jnp.stack([z, z & 1, z >> 1, dp])
    block, group = query_proj.shape[1:]
    quarter, length = filter_taps.shape
    half = length // 2
    rows = quarter // 2
    table = as_const(dft_table(length))
    macs = length * half * quarter

    def xz(vals, k):
        return lax.ppermute(vals, "ctx", [(i, i ^ k) for i in range(4)])

    def xd(vals, k):
        return lax.ppermute(vals, "dp", [(i, i ^ k) for i in range(4)])

    def apart(run, *args):
        shapes = jax.eval_shape(run, *args)
        return lax.cond(dp >= 0, run, lambda *_: jax.tree.map(lambda s: jnp.zeros(s.shape, s.dtype), shapes), *args)

    def over_cores(keep, send):
        return (keep.astype(f32) + xd(send, 1).astype(f32)).astype(bf16)

    share = quarter // 2
    one, two, spec = ((block, quarter), bf16), ((2, block, quarter), bf16), ((length, quarter), bf16)
    act_in = ((1, block, group), lambda i, idx: (0, 0, 0))
    two_out = ((2, block, quarter), lambda i, idx: (0, 0, 0)) + two
    one_out = ((block, quarter), lambda i, idx: (0, 0)) + one
    gate_ins = [act_in] * 4 + [((share, half), lambda i, idx: (idx[3] & 1, 0))]
    gate_outs = [two_out] * 4 + [one_out] * 2 + [((share, half), lambda i, idx: (0, 0), (share, half), bf16)]
    keep_own, keep_far, own1, far1, to2, to3, piece = pl.pallas_call(
        functools.partial(gate_kernel, quarter),
        out_shape=[jax.ShapeDtypeStruct(s, d) for _, _, s, d in gate_outs],
        grid_spec=pltpu.PrefetchScalarGridSpec(
            num_scalar_prefetch=1,
            grid=(1,),
            in_specs=[pl.BlockSpec(blk, at) for blk, at in gate_ins],
            out_specs=[pl.BlockSpec(blk, at) for blk, at, _, _ in gate_outs],
        ),
        compiler_params=pltpu.CompilerParams(vmem_limit_bytes=GATE_VMEM),
        cost_estimate=pl.CostEstimate(flops=2 * block * group, bytes_accessed=16 * block * group, transcendentals=0),
    )(idx, query_proj, key_proj, value_proj, out_grad, filter_taps)
    piece = xz(piece, 2)
    near, cross, inv = call(
        own_filter_kernel, [spec] * 2 + [((half, length), bf16)], 2, smem_first=False, cost=(6 * macs, 16 * length * quarter)
    )(table, filter_taps)
    near, cross, inv, piece = lax.optimization_barrier((near, cross, inv, piece))
    other_piece = xd(piece, 1)
    far1, to2, to3, own1 = xz(far1, 1), xz(to2, 2), xz(to3, 3), xz(own1, 1)

    def far_quarter(idx, inv, piece, other_piece, keep_far, far1):
        okeep, o1, *parts = call(
            conv_far_kernel,
            [two] * 2 + [((rows, half), bf16)] * 2,
            6,
            cost=(8 * macs, 32 * length * quarter),
            limit=CONV_VMEM,
            scratch=[pltpu.VMEM((length, quarter), f32), pltpu.VMEM((length, quarter), bf16), pltpu.VMEM((4, half, quarter), bf16)],
        )(idx, table, inv, piece, other_piece, keep_far, far1)
        return okeep, o1, over_cores(*parts)

    okeep_far, ofar1, far = apart(far_quarter, idx, inv, piece, other_piece, keep_far, far1)
    ofar1 = xz(ofar1, 1)
    far, cross = lax.optimization_barrier((far, cross))
    far = xz(far, 2)
    o2, o3 = call(
        cross_kernel, [one] * 2, 5, cost=(4 * macs, 8 * length * quarter), scratch=[pltpu.VMEM((2, half, quarter), bf16)]
    )(idx, table, inv, cross, keep_own, own1)
    o2, o3 = xz(o2, 2), xz(o3, 3)
    own_parts = call(
        own_filter_grad_kernel,
        [((rows, length), bf16)] * 2,
        5,
        in_hbm=2,
        cost=(48 * macs, 32 * length * quarter),
        limit=CONV_VMEM,
        scratch=[pltpu.VMEM((length, quarter), bf16)] * 2
        + [pltpu.VMEM((3, half, quarter), bf16), pltpu.SemaphoreType.DMA((2,))],
    )(idx, to2, to3, table, keep_own, own1)

    def own_quarter(own_parts, far, idx, *conv_ins):
        chip = own_parts[0].astype(f32) + xd(own_parts[1], 1).astype(f32)
        chip = jnp.concatenate([chip[:, :half] + far.astype(f32), chip[:, half:]], 1)
        chip = lax.reduce_precision(chip, 8, 7).astype(bf16)
        theirs = xd(chip, 2)
        okeep, o1 = call(
            conv_own_kernel,
            [two] * 2,
            8,
            in_hbm=2,
            cost=(4 * macs, 4 * length * quarter),
            limit=CONV_VMEM,
            scratch=[pltpu.VMEM((5, half, quarter), bf16), pltpu.SemaphoreType.DMA((2,))],
        )(idx, *conv_ins)
        o1 = xz(o1, 1)

        def both_cores(chip, theirs):
            mine = (chip.astype(f32) + theirs.astype(f32)).astype(bf16)
            return mine, xd(mine, 1)

        return okeep, o1, *apart(both_cores, chip, theirs)

    okeep, o1, mine, other = apart(
        own_quarter, own_parts, far, idx, to2, to3, table, inv, near, cross, keep_own, own1
    )
    act = (query_proj.shape, bf16)
    return call(
        functools.partial(final_kernel, quarter),
        [act] * 3 + [(filter_taps.shape, f32)],
        11,
        out_hbm=True,
        cost=(3 * block * group, 18 * block * group),
        scratch=[
            pltpu.VMEM((3, block, group), bf16),
            pltpu.VMEM(filter_taps.shape, f32),
            pltpu.SemaphoreType.DMA((3 * ROW_CHUNKS + 2 * FILT_CHUNKS,)),
        ],
    )(idx, query_proj, key_proj, out_grad, okeep, okeep_far, o1, ofar1, o2, o3, mine, other)


exact_mode = lax.Precision.HIGHEST
field_mode = lax.Precision.HIGH


def factor_sizes(length):
    col_count = min(128, length)
    return (2 * length // col_count, col_count)


def angle_table(first_size, second_size, period):
    product = (
        jnp.arange(first_size, dtype=jnp.int32)[:, None]
        * jnp.arange(second_size, dtype=jnp.int32)[None, :]
        % period
    )
    angles = product.astype(jnp.float32) * (2.0 * math.pi / period)
    return (jnp.cos(angles), jnp.sin(angles))


def make_tables(length):
    row_count, col_count = factor_sizes(length)
    outer_cos, outer_sin = angle_table(row_count, row_count // 2, row_count)
    twist_cos, twist_sin = angle_table(row_count, col_count, row_count * col_count)
    inner_cos, inner_sin = angle_table(col_count, col_count, col_count)
    real_outer = jnp.stack([outer_cos, -outer_sin])
    mixed_outer = jnp.stack([jnp.stack([outer_cos, outer_sin]), jnp.stack([-outer_sin, outer_cos])])
    fwd_twist = jnp.stack([twist_cos, -twist_sin])[:, None]
    inv_twist = jnp.stack([twist_cos, twist_sin])[:, None]
    fwd_inner = jnp.stack([jnp.stack([inner_cos, -inner_sin]), jnp.stack([inner_sin, inner_cos])])
    inv_inner = jnp.stack([jnp.stack([inner_cos, inner_sin]), jnp.stack([-inner_sin, inner_cos])])
    back_outer = jnp.stack([outer_cos, -outer_sin]) / float(row_count * col_count)
    return (real_outer, mixed_outer, fwd_twist, inv_twist, fwd_inner, inv_inner, back_outer)


def complex_mul(left, right):
    return jnp.stack(
        [left[0] * right[0] - left[1] * right[1], left[0] * right[1] + left[1] * right[0]]
    )


def conjugate(values):
    return jnp.stack([values[0], -values[1]])


def forward(values, tables, mode):
    real_outer, mixed_outer, fwd_twist, inv_twist, fwd_inner, inv_inner, back_outer = tables
    half_rows = real_outer.shape[2]
    col_count = fwd_inner.shape[2]
    grid = values.reshape(values.shape[0], half_rows, col_count)
    first = jnp.einsum("sca,hab->shcb", real_outer, grid, precision=mode)
    turned = complex_mul(first, fwd_twist)
    return jnp.einsum("shcb,stbd->thcd", turned, fwd_inner, precision=mode)


def inverse(spectrum, tables, mode):
    real_outer, mixed_outer, fwd_twist, inv_twist, fwd_inner, inv_inner, back_outer = tables
    back = jnp.einsum("shcd,stdb->thcb", spectrum, inv_inner, precision=mode)
    turned = complex_mul(back, inv_twist)
    out_grid = jnp.einsum("sca,shcb->hab", back_outer, turned, precision=mode)
    return out_grid.reshape(out_grid.shape[0], -1)


def whole_plan(query_proj, key_proj, value_proj, out_grad, filter_taps):
    query_vals = query_proj[0].astype(jnp.float32)
    key_vals = key_proj[0].astype(jnp.float32)
    grad_vals = out_grad[0].astype(jnp.float32)
    gated_vals = (query_vals * key_vals).astype(jnp.bfloat16).T
    grad_conv = (grad_vals * value_proj[0].astype(jnp.float32)).astype(jnp.bfloat16).T
    length = filter_taps.shape[1]
    tables = make_tables(length)
    filt_spec = forward(filter_taps, tables, exact_mode)
    gated_all = lax.all_to_all(gated_vals, "ctx", split_axis=0, concat_axis=1, tiled=True)
    gate_spec = forward(gated_all.astype(jnp.float32), tables, field_mode)
    conv_full = inverse(complex_mul(gate_spec, filt_spec), tables, field_mode).astype(jnp.bfloat16)
    conv_local = lax.all_to_all(conv_full, "ctx", split_axis=1, concat_axis=0, tiled=True)
    grad_all = lax.all_to_all(grad_conv, "ctx", split_axis=0, concat_axis=1, tiled=True)
    grad_spec = forward(grad_all.astype(jnp.float32), tables, field_mode)
    back_full = inverse(complex_mul(grad_spec, conjugate(filt_spec)), tables, field_mode).astype(
        jnp.bfloat16
    )
    back_local = lax.all_to_all(back_full, "ctx", split_axis=1, concat_axis=0, tiled=True)
    grad_v = (grad_vals * conv_local.T.astype(jnp.float32)).astype(jnp.bfloat16)[None]
    back_vals = back_local.T.astype(jnp.float32)
    grad_q = (back_vals * key_vals).astype(jnp.bfloat16)[None]
    grad_k = (back_vals * query_vals).astype(jnp.bfloat16)[None]
    cross_spec = complex_mul(conjugate(gate_spec), grad_spec)
    grad_filt = lax.psum(inverse(cross_spec, tables, exact_mode).astype(jnp.bfloat16), "dp").astype(
        jnp.float32
    )
    return (grad_q, grad_k, grad_v, grad_filt)

def solution(mesh):
    split = mesh.shape["ctx"] == 4 and mesh.shape["dp"] == 4
    body = half_plan if split else whole_plan
    acts = P("dp", "ctx", "chan")
    taps = P(("chan", "ctx"), None)
    return jax.shard_map(
        body,
        mesh=mesh,
        in_specs=(acts, acts, acts, acts, taps),
        out_specs=(acts, acts, acts, taps),
        check_vma=False,
    )
```

```python
import functools
import math

import jax
import jax.numpy as jnp
import ml_dtypes
import numpy as np
from jax import lax
from jax.experimental import pallas as pl
from jax.experimental.pallas import tpu as pltpu
from jax.sharding import PartitionSpec as P

bf16 = jnp.bfloat16
f32 = jnp.float32
VMEM_LIMIT = 20 * 1024 * 1024
CONV_VMEM = 20 * 1024 * 1024
GATE_VMEM = 58 * 1024 * 1024
ROW_CHUNKS = 2
FILT_CHUNKS = 4


def dft_table(size):
    freq = np.arange(size // 2)[:, None]
    pos = np.arange(-size // 2, size // 2)[None, :]
    angle = 2.0 * np.pi * (((2 * freq + 1) * pos) % (2 * size)) / (2 * size)
    return np.concatenate([np.cos(angle), -np.sin(angle)], 0)


def as_const(table):
    return jnp.asarray(np.ascontiguousarray(table).astype(ml_dtypes.bfloat16))


def mm(left, right, dims=((1,), (0,))):
    return lax.dot_general(left, right, (dims, ((), ())), preferred_element_type=f32)


def cmul(left, right):
    half = left.shape[0] // 2
    lr, li, rr, ri = left[:half], left[half:], right[:half], right[half:]
    return lr * rr - li * ri, lr * ri + li * rr


def cmulc(left, right):
    half = left.shape[0] // 2
    lr, li, rr, ri = left[:half], left[half:], right[:half], right[half:]
    return lr * rr + li * ri, lr * ri - li * rr


def join(pair):
    return jnp.concatenate([pair[0], pair[1]], 0)


def lanes(start, width):
    return pl.ds(pl.multiple_of(start, 128), width)


def call(kernel, outs, n_in, smem_first=True, cost=(0, 0), limit=VMEM_LIMIT, in_hbm=0, out_hbm=False, scratch=()):
    vmem, hbm = pl.BlockSpec(memory_space=pltpu.VMEM), pl.BlockSpec(memory_space=pl.ANY)
    in_specs = [hbm] * in_hbm + [vmem] * (n_in - in_hbm)
    if smem_first:
        in_specs = [pl.BlockSpec(memory_space=pltpu.SMEM)] + in_specs
    return pl.pallas_call(
        kernel,
        out_shape=[jax.ShapeDtypeStruct(s, d) for s, d in outs],
        in_specs=in_specs,
        out_specs=[hbm if out_hbm else vmem] * len(outs),
        scratch_shapes=scratch,
        compiler_params=pltpu.CompilerParams(vmem_limit_bytes=limit),
        cost_estimate=pl.CostEstimate(flops=cost[0], bytes_accessed=cost[1], transcendentals=0),
    )


def gate_kernel(quarter, idx, q, k, v, g, taps, keep_own, keep_far, own1, far1, to2, to3, piece):
    z, upper = idx[0], idx[2]
    piece[...] = taps[...].astype(bf16)
    for r, dest in ((3, far1), (2, keep_far), (1, own1), (0, keep_own)):
        cols = lanes((z ^ r) * quarter, quarter)
        gated = (q[0, :, cols].astype(f32) * k[0, :, cols].astype(f32)).astype(bf16)
        grad = (g[0, :, cols].astype(f32) * v[0, :, cols].astype(f32)).astype(bf16)
        dest[0] = gated
        dest[1] = grad
        if r >= 2:
            sel = jnp.where(upper == 0, gated.astype(f32), grad.astype(f32)).astype(bf16)
            (to2 if r == 2 else to3)[...] = sel


def own_filter_kernel(table, taps, near, cross, inv):
    half = taps.shape[1] // 2
    inv[...] = (table[:, half:].astype(f32).T * (1.0 / half)).astype(bf16)
    vals = taps[...].astype(bf16)
    cross[...] = mm(table[...], vals, ((1,), (1,))).astype(bf16)
    near[...] = mm(table[:, half:], vals[:, :half], ((1,), (1,))).astype(bf16)


def in_order(low, mine, partner, held):
    block = mine.shape[0]
    held[pl.ds(pl.multiple_of(low * block, block), block), :] = mine
    held[pl.ds(pl.multiple_of((1 - low) * block, block), block), :] = partner
    return held[...]


def forward_two(fwd, first, second):
    both = mm(fwd, jnp.concatenate([first, second], 1))
    width = first.shape[1]
    return both[:, :width], both[:, width:]


def halves(low, vals, held, mine, partner):
    held[...] = vals
    block = vals.shape[0] // 2
    mine[...] = held[pl.ds(pl.multiple_of(low * block, block), block), :]
    partner[...] = held[pl.ds(pl.multiple_of((1 - low) * block, block), block), :]


def filt_part(core, table, terms, keep, send):
    half = table.shape[1] // 2
    width = keep.shape[0]
    for dest, which in ((send, 1 - core), (keep, core)):
        cols = lanes(which * width, width)
        for first, pairs in terms:
            vals = sum(mm(q[:, cols], table[:, start : start + half], ((0,), (0,))) for q, start in pairs)
            dest[:, first : first + half] = (vals * (1.0 / half)).astype(dest.dtype)


def conv_far_kernel(idx, table, inv, mine, other, keep, recv, okeep, o1, gkeep, gsend, filt, q_far, held):
    low, core = idx[1], idx[3] & 1
    half = table.shape[1] // 2
    share = mine.shape[0]
    fwd = table[:, half:]
    x, g = forward_two(fwd, in_order(low, keep[0], recv[0], held.at[0]), in_order(low, keep[1], recv[1], held.at[1]))
    for which, piece in ((core, mine), (1 - core, other)):
        filt[:, lanes(which * share, share)] = mm(fwd, piece[...], ((1,), (1,)))
    h = filt[...]
    q_far[...] = join(cmulc(x, g)).astype(bf16)
    for kind, pair in ((0, cmul(x, h)), (1, cmulc(h, g))):
        halves(low, mm(inv[...], join(pair).astype(bf16)).astype(bf16), held.at[2 + kind], okeep.at[kind], o1.at[kind])
    filt_part(core, table, [(0, [(q_far, half)])], gkeep, gsend)


def cross_kernel(idx, table, inv, cross, keep, recv, o2, o3, held):
    low, upper = idx[1], idx[2]
    half = table.shape[1] // 2
    spec = mm(table[:, half:], in_order(low, keep[upper], recv[upper], held.at[0]))
    h = cross[...].astype(f32)
    sign = jnp.where(upper == 0, 1.0, -1.0)
    pair = cmul(jnp.concatenate([h[:half], h[half:] * sign], 0), spec)
    halves(low, mm(inv[...], join(pair).astype(bf16)).astype(bf16), held.at[1], o2, o3)


def load_blocks(low, r2, r3, held, sems):
    block = r2.shape[0]
    loads = []
    for j, (src, place) in enumerate(((r2, low), (r3, 1 - low))):
        at = pl.ds(pl.multiple_of(place * block, block), block)
        loads.append(pltpu.make_async_copy(src, held.at[at], sems.at[j]))
        loads[j].start()
    return loads


def own_filter_grad_kernel(idx, r2, r3, table, keep, recv, gkeep, gsend, q_near, q_cross, held, sems):
    low, upper, core = idx[1], idx[2], idx[3] & 1
    half = table.shape[1] // 2
    loads = load_blocks(low, r2, r3, held.at[2], sems)
    fwd = table[:, half:]
    x, g = forward_two(fwd, in_order(low, keep[0], recv[0], held.at[0]), in_order(low, keep[1], recv[1], held.at[1]))
    q_near[...] = join(cmulc(x, g)).astype(bf16)
    for load in loads:
        load.wait()
    rec = mm(fwd, held[2])

    def lower():
        q_cross[...] = join(cmulc(x, rec)).astype(bf16)

    def higher():
        q_cross[...] = join(cmulc(rec, g)).astype(bf16)

    pl.when(upper == 0)(lower)
    pl.when(upper != 0)(higher)
    filt_part(core, table, [(0, [(q_cross, 0), (q_near, half)]), (half, [(q_cross, half)])], gkeep, gsend)


def conv_own_kernel(idx, r2, r3, table, inv, near, cross, keep, recv, okeep, o1, held, sems):
    low, upper = idx[1], idx[2]
    half = table.shape[1] // 2
    loads = load_blocks(low, r2, r3, held.at[2], sems)
    fwd = table[:, half:]
    x, g = forward_two(fwd, in_order(low, keep[0], recv[0], held.at[0]), in_order(low, keep[1], recv[1], held.at[1]))
    h = near[...].astype(f32)
    hx = cross[...].astype(f32)
    for load in loads:
        load.wait()
    rec = mm(fwd, held[2])

    def put(conv, back):
        width = x.shape[1]
        both = jnp.concatenate([join(conv).astype(bf16), join(back).astype(bf16)], 1)
        vals = mm(inv[...], both).astype(bf16)
        halves(low, vals[:, :width], held.at[3], okeep.at[0], o1.at[0])
        halves(low, vals[:, width:], held.at[4], okeep.at[1], o1.at[1])

    def lower():
        back, add = cmulc(h, g), cmulc(hx, rec)
        put(cmul(x, h), (back[0] + add[0], back[1] + add[1]))

    def higher():
        conv, add = cmul(x, h), cmul(hx, rec)
        put((conv[0] + add[0], conv[1] + add[1]), cmulc(h, g))

    pl.when(upper == 0)(lower)
    pl.when(upper != 0)(higher)


def final_kernel(quarter, idx, q, k, g, own, far, own1, far1, r2, r3, mine, other, dq, dk, dv, grad_filt, held, filt_held, sems):
    z, upper, core = idx[0], idx[2], idx[3] & 1
    is_up = jnp.where(upper == 0, 0.0, 1.0)
    size = mine.shape[0]
    part_size = size // FILT_CHUNKS
    copies = []
    for which, piece in ((core, mine), (1 - core, other)):
        for j in range(FILT_CHUNKS):
            at = pl.ds(pl.multiple_of(which * size + j * part_size, 8), part_size)
            filt_held[at, :] = piece[j * part_size : (j + 1) * part_size, :].astype(f32)
            copies.append(pltpu.make_async_copy(filt_held.at[at], grad_filt.at[at], sems.at[3 * ROW_CHUNKS + len(copies)]))
            copies[-1].start()
    rows = q.shape[1] // ROW_CHUNKS
    for c in range(ROW_CHUNKS):
        part = pl.ds(c * rows, rows)
        for r, src in enumerate((own, own1, far, far1)):
            cols = lanes((z ^ r) * quarter, quarter)
            conv = src[0, part].astype(f32)
            back = src[1, part].astype(f32)
            if r >= 2:
                add = (r2 if r == 2 else r3)[part].astype(f32)
                conv = conv + is_up * add
                back = back + (1.0 - is_up) * add
            held[0, part, cols] = (back * k[0, part, cols].astype(f32)).astype(bf16)
            held[1, part, cols] = (back * q[0, part, cols].astype(f32)).astype(bf16)
            held[2, part, cols] = (g[0, part, cols].astype(f32) * conv).astype(bf16)
        for j, dest in enumerate((dq, dk, dv)):
            copies.append(pltpu.make_async_copy(held.at[j, part], dest.at[0, part], sems.at[3 * c + j]))
            copies[-1].start()
    for copy in copies:
        copy.wait()


def half_plan(query_proj, key_proj, value_proj, out_grad, filter_taps):
    z = lax.axis_index("ctx").astype(jnp.int32)
    dp = lax.axis_index("dp").astype(jnp.int32)
    idx = jnp.stack([z, z & 1, z >> 1, dp])
    block, group = query_proj.shape[1:]
    quarter, length = filter_taps.shape
    half = length // 2
    rows = quarter // 2
    table = as_const(dft_table(length))
    macs = length * half * quarter

    def xz(vals, k):
        return lax.ppermute(vals, "ctx", [(i, i ^ k) for i in range(4)])

    def xd(vals, k):
        return lax.ppermute(vals, "dp", [(i, i ^ k) for i in range(4)])

    def apart(run, *args):
        shapes = jax.eval_shape(run, *args)
        return lax.cond(dp >= 0, run, lambda *_: jax.tree.map(lambda s: jnp.zeros(s.shape, s.dtype), shapes), *args)

    def over_cores(keep, send):
        return (keep.astype(f32) + xd(send, 1).astype(f32)).astype(bf16)

    share = quarter // 2
    one, two, spec = ((block, quarter), bf16), ((2, block, quarter), bf16), ((length, quarter), bf16)
    act_in = ((1, block, group), lambda i, idx: (0, 0, 0))
    two_out = ((2, block, quarter), lambda i, idx: (0, 0, 0)) + two
    one_out = ((block, quarter), lambda i, idx: (0, 0)) + one
    gate_ins = [act_in] * 4 + [((share, half), lambda i, idx: (idx[3] & 1, 0))]
    gate_outs = [two_out] * 4 + [one_out] * 2 + [((share, half), lambda i, idx: (0, 0), (share, half), bf16)]
    keep_own, keep_far, own1, far1, to2, to3, piece = pl.pallas_call(
        functools.partial(gate_kernel, quarter),
        out_shape=[jax.ShapeDtypeStruct(s, d) for _, _, s, d in gate_outs],
        grid_spec=pltpu.PrefetchScalarGridSpec(
            num_scalar_prefetch=1,
            grid=(1,),
            in_specs=[pl.BlockSpec(blk, at) for blk, at in gate_ins],
            out_specs=[pl.BlockSpec(blk, at) for blk, at, _, _ in gate_outs],
        ),
        compiler_params=pltpu.CompilerParams(vmem_limit_bytes=GATE_VMEM),
        cost_estimate=pl.CostEstimate(flops=2 * block * group, bytes_accessed=16 * block * group, transcendentals=0),
    )(idx, query_proj, key_proj, value_proj, out_grad, filter_taps)
    piece = xz(piece, 2)
    near, cross, inv = call(
        own_filter_kernel, [spec] * 2 + [((half, length), bf16)], 2, smem_first=False, cost=(6 * macs, 16 * length * quarter)
    )(table, filter_taps)
    near, cross, inv, piece = lax.optimization_barrier((near, cross, inv, piece))
    other_piece = xd(piece, 1)
    far1, to2, to3, own1 = xz(far1, 1), xz(to2, 2), xz(to3, 3), xz(own1, 1)

    def far_quarter(idx, inv, piece, other_piece, keep_far, far1):
        okeep, o1, *parts = call(
            conv_far_kernel,
            [two] * 2 + [((rows, half), bf16)] * 2,
            6,
            cost=(8 * macs, 32 * length * quarter),
            limit=CONV_VMEM,
            scratch=[pltpu.VMEM((length, quarter), f32), pltpu.VMEM((length, quarter), bf16), pltpu.VMEM((4, half, quarter), bf16)],
        )(idx, table, inv, piece, other_piece, keep_far, far1)
        return okeep, o1, over_cores(*parts)

    okeep_far, ofar1, far = apart(far_quarter, idx, inv, piece, other_piece, keep_far, far1)
    ofar1 = xz(ofar1, 1)
    far, cross = lax.optimization_barrier((far, cross))
    far = xz(far, 2)
    o2, o3 = call(
        cross_kernel, [one] * 2, 5, cost=(4 * macs, 8 * length * quarter), scratch=[pltpu.VMEM((2, half, quarter), bf16)]
    )(idx, table, inv, cross, keep_own, own1)
    o2, o3 = xz(o2, 2), xz(o3, 3)
    own_parts = call(
        own_filter_grad_kernel,
        [((rows, length), bf16)] * 2,
        5,
        in_hbm=2,
        cost=(48 * macs, 32 * length * quarter),
        limit=CONV_VMEM,
        scratch=[pltpu.VMEM((length, quarter), bf16)] * 2
        + [pltpu.VMEM((3, half, quarter), bf16), pltpu.SemaphoreType.DMA((2,))],
    )(idx, to2, to3, table, keep_own, own1)

    def own_quarter(own_parts, far, idx, *conv_ins):
        chip = own_parts[0].astype(f32) + xd(own_parts[1], 1).astype(f32)
        chip = jnp.concatenate([chip[:, :half] + far.astype(f32), chip[:, half:]], 1)
        chip = lax.reduce_precision(chip, 8, 7).astype(bf16)
        theirs = xd(chip, 2)
        okeep, o1 = call(
            conv_own_kernel,
            [two] * 2,
            8,
            in_hbm=2,
            cost=(4 * macs, 4 * length * quarter),
            limit=CONV_VMEM,
            scratch=[pltpu.VMEM((5, half, quarter), bf16), pltpu.SemaphoreType.DMA((2,))],
        )(idx, *conv_ins)
        o1 = xz(o1, 1)

        def both_cores(chip, theirs):
            mine = (chip.astype(f32) + theirs.astype(f32)).astype(bf16)
            return mine, xd(mine, 1)

        return okeep, o1, *apart(both_cores, chip, theirs)

    okeep, o1, mine, other = apart(
        own_quarter, own_parts, far, idx, to2, to3, table, inv, near, cross, keep_own, own1
    )
    act = (query_proj.shape, bf16)
    return call(
        functools.partial(final_kernel, quarter),
        [act] * 3 + [(filter_taps.shape, f32)],
        11,
        out_hbm=True,
        cost=(3 * block * group, 18 * block * group),
        scratch=[
            pltpu.VMEM((3, block, group), bf16),
            pltpu.VMEM(filter_taps.shape, f32),
            pltpu.SemaphoreType.DMA((3 * ROW_CHUNKS + 2 * FILT_CHUNKS,)),
        ],
    )(idx, query_proj, key_proj, out_grad, okeep, okeep_far, o1, ofar1, o2, o3, mine, other)


exact_mode = lax.Precision.HIGHEST
field_mode = lax.Precision.HIGH


def factor_sizes(length):
    col_count = min(128, length)
    return (2 * length // col_count, col_count)


def angle_table(first_size, second_size, period):
    product = (
        jnp.arange(first_size, dtype=jnp.int32)[:, None]
        * jnp.arange(second_size, dtype=jnp.int32)[None, :]
        % period
    )
    angles = product.astype(jnp.float32) * (2.0 * math.pi / period)
    return (jnp.cos(angles), jnp.sin(angles))


def make_tables(length):
    row_count, col_count = factor_sizes(length)
    outer_cos, outer_sin = angle_table(row_count, row_count // 2, row_count)
    twist_cos, twist_sin = angle_table(row_count, col_count, row_count * col_count)
    inner_cos, inner_sin = angle_table(col_count, col_count, col_count)
    real_outer = jnp.stack([outer_cos, -outer_sin])
    mixed_outer = jnp.stack([jnp.stack([outer_cos, outer_sin]), jnp.stack([-outer_sin, outer_cos])])
    fwd_twist = jnp.stack([twist_cos, -twist_sin])[:, None]
    inv_twist = jnp.stack([twist_cos, twist_sin])[:, None]
    fwd_inner = jnp.stack([jnp.stack([inner_cos, -inner_sin]), jnp.stack([inner_sin, inner_cos])])
    inv_inner = jnp.stack([jnp.stack([inner_cos, inner_sin]), jnp.stack([-inner_sin, inner_cos])])
    back_outer = jnp.stack([outer_cos, -outer_sin]) / float(row_count * col_count)
    return (real_outer, mixed_outer, fwd_twist, inv_twist, fwd_inner, inv_inner, back_outer)


def complex_mul(left, right):
    return jnp.stack(
        [left[0] * right[0] - left[1] * right[1], left[0] * right[1] + left[1] * right[0]]
    )


def conjugate(values):
    return jnp.stack([values[0], -values[1]])


def forward(values, tables, mode):
    real_outer, mixed_outer, fwd_twist, inv_twist, fwd_inner, inv_inner, back_outer = tables
    half_rows = real_outer.shape[2]
    col_count = fwd_inner.shape[2]
    grid = values.reshape(values.shape[0], half_rows, col_count)
    first = jnp.einsum("sca,hab->shcb", real_outer, grid, precision=mode)
    turned = complex_mul(first, fwd_twist)
    return jnp.einsum("shcb,stbd->thcd", turned, fwd_inner, precision=mode)


def inverse(spectrum, tables, mode):
    real_outer, mixed_outer, fwd_twist, inv_twist, fwd_inner, inv_inner, back_outer = tables
    back = jnp.einsum("shcd,stdb->thcb", spectrum, inv_inner, precision=mode)
    turned = complex_mul(back, inv_twist)
    out_grid = jnp.einsum("sca,shcb->hab", back_outer, turned, precision=mode)
    return out_grid.reshape(out_grid.shape[0], -1)


def whole_plan(query_proj, key_proj, value_proj, out_grad, filter_taps):
    query_vals = query_proj[0].astype(jnp.float32)
    key_vals = key_proj[0].astype(jnp.float32)
    grad_vals = out_grad[0].astype(jnp.float32)
    gated_vals = (query_vals * key_vals).astype(jnp.bfloat16).T
    grad_conv = (grad_vals * value_proj[0].astype(jnp.float32)).astype(jnp.bfloat16).T
    length = filter_taps.shape[1]
    tables = make_tables(length)
    filt_spec = forward(filter_taps, tables, exact_mode)
    gated_all = lax.all_to_all(gated_vals, "ctx", split_axis=0, concat_axis=1, tiled=True)
    gate_spec = forward(gated_all.astype(jnp.float32), tables, field_mode)
    conv_full = inverse(complex_mul(gate_spec, filt_spec), tables, field_mode).astype(jnp.bfloat16)
    conv_local = lax.all_to_all(conv_full, "ctx", split_axis=1, concat_axis=0, tiled=True)
    grad_all = lax.all_to_all(grad_conv, "ctx", split_axis=0, concat_axis=1, tiled=True)
    grad_spec = forward(grad_all.astype(jnp.float32), tables, field_mode)
    back_full = inverse(complex_mul(grad_spec, conjugate(filt_spec)), tables, field_mode).astype(
        jnp.bfloat16
    )
    back_local = lax.all_to_all(back_full, "ctx", split_axis=1, concat_axis=0, tiled=True)
    grad_v = (grad_vals * conv_local.T.astype(jnp.float32)).astype(jnp.bfloat16)[None]
    back_vals = back_local.T.astype(jnp.float32)
    grad_q = (back_vals * key_vals).astype(jnp.bfloat16)[None]
    grad_k = (back_vals * query_vals).astype(jnp.bfloat16)[None]
    cross_spec = complex_mul(conjugate(gate_spec), grad_spec)
    grad_filt = lax.psum(inverse(cross_spec, tables, exact_mode).astype(jnp.bfloat16), "dp").astype(
        jnp.float32
    )
    return (grad_q, grad_k, grad_v, grad_filt)

def solution(mesh):
    split = mesh.shape["ctx"] == 4 and mesh.shape["dp"] == 4
    body = half_plan if split else whole_plan
    acts = P("dp", "ctx", "chan")
    taps = P(("chan", "ctx"), None)
    return jax.shard_map(
        body,
        mesh=mesh,
        in_specs=(acts, acts, acts, acts, taps),
        out_specs=(acts, acts, acts, taps),
        check_vma=False,
    )
```
